128 devices in a mesh: px: 8 (over x, core), py: 16 (over z, y).
Axes of the slice: x: 4, y: 4, z: 4, core: 2. Of those that a mesh axis runs over, the one named last changes fastest.
Arguments:
- displacement: float32 [3, 524288], P(None, ('px', 'py')), may hold values from -6 to 6
- disp_prev: float32 [3, 524288], P(None, ('px', 'py')), may hold values from -6 to 6
- nodal_load: float32 [3, 524288], P(None, ('px', 'py')), may hold values from -6 to 6
- nodal_mass: float32 [524288], P(('px', 'py')), may hold values from 1 to 4
- modulus: float32 [65536], P(('px', 'py')), may hold values from 1 to 10
- stiffness: float32 [81, 81], replicated
- connectivity: int32 [27, 65536], P(None, ('px', 'py')), may hold values from 0 to 4607, as said below
- ghost_send: int32 [2, 32768], P(None, ('px', 'py')), may hold values from 0 to 4095
- contact_node: int32 [262144], P(('px', 'py')), may hold values from 0 to 4095
- contact_owner: int32 [262144], P(('px', 'py')), may hold values from 0 to 127, as said below
- pair_ids: int32 [2, 131072], P(None, ('px', 'py')), may hold values from 0 to 4095
- gap_start: float32 [3, 131072], P(None, ('px', 'py')), may hold values from -3 to 3
- penalty: float32 [131072], P(('px', 'py')), may hold values from 0.5 to 2
- friction: float32 [131072], P(('px', 'py')), may hold values from 0.2 to 0.6
- slip_state: int32 [3, 131072], P(None, ('px', 'py')), may hold values 0 or 1
Outputs:
- new_displacement: float32 [3, 524288], P(None, ('px', 'py'))
- acceleration: float32 [3, 524288], P(None, ('px', 'py'))
The draws below stay inside these ranges and needn't reach their ends.
Inputs may be any that keep to these rules, and one draw needn't show every extreme that they name: `connectivity`: of each device's 512 elements, the first 384 name only the device's own nodes, indices below 4096; the others name own and ghost nodes. `contact_owner`: among the 2048 contact nodes of one device at most 32 name the same owner; one owner is named by exactly 32 nodes of every device.
All inputs are finite; a program needn't handle non-finite values. No bound on the sum of `slip_state` on one device may be relied on, other than what follows from the above.
Results may differ from the reference program's by a relative error of at most 0.0003.
Values sent between devices are 32-bit elements; how exact they have to be, the bound alone decides.
No kernel may reach another device: no remote copies, remote signals or barrier semaphores. Data moves between devices by JAX's collectives and lax.ppermute only.
A program may use at most 64 MiB of HBM per device.

```python
import math
import jax
import jax.numpy as jnp
from jax import lax

ELNODE = 27
ELDOF = 81
STEPS = 3
NODE_DEV = 4096
NE_DEV = 512
HB = 256
CN_DEV = 2048
PAIRS_PER_OWNER = 1024
NE_IN = 384
OWNER_TOTAL = 128
CAP = 32
NODES = 524288
ELEMS = 65536
GHOSTS = 32768
CONTACT = 262144
PAIRS = 131072


def draw_stiffness(key, part):
    key_coupling, key_diagonal = jax.random.split(key)
    random_part = jax.random.uniform(key_coupling, (ELDOF, ELDOF), jnp.float32, -1.0, 1.0)
    diagonal = jax.random.uniform(key_diagonal, (ELDOF,), jnp.float32, 1.2, 1.6)
    coupling = 0.06 * (random_part + random_part.T)
    identity = jnp.eye(ELDOF, dtype=jnp.float32)
    return 0.05 * (coupling * (1.0 - identity) + jnp.diag(diagonal))


def draw_connectivity(key, part):
    key_any, key_own = jax.random.split(key)
    anywhere = jax.random.randint(key_any, (ELNODE, OWNER_TOTAL, NE_DEV), 0, NODE_DEV + 2 * HB)
    own_only = jax.random.randint(key_own, (ELNODE, OWNER_TOTAL, NE_DEV), 0, NODE_DEV)
    column = jnp.arange(NE_DEV)[None, None, :]
    chosen = jnp.where(column < NE_IN, own_only, anywhere)
    return chosen.reshape(ELNODE, OWNER_TOTAL * NE_DEV).astype(jnp.int32)


def draw_contact_owner(key, part):
    key_star, key_pick, key_order = jax.random.split(key, 3)
    favored = jax.random.randint(key_star, (), 0, OWNER_TOTAL)
    total_slots = OWNER_TOTAL * CAP
    pick_keys = jax.random.split(key_pick, OWNER_TOTAL)
    order_keys = jax.random.split(key_order, OWNER_TOTAL)

    def one_device(pick_key, order_key):
        scores = jax.random.permutation(pick_key, total_slots)
        slot_owner = jnp.arange(total_slots) // CAP
        scores = scores + jnp.where(slot_owner == favored, total_slots, 0)
        top_values, chosen = lax.top_k(scores, CN_DEV)
        chosen = jax.random.permutation(order_key, chosen)
        return (chosen // CAP).astype(jnp.int32)
    return jax.vmap(one_device)(pick_keys, order_keys).reshape(OWNER_TOTAL * CN_DEV).astype(jnp.int32)


def with_ends(values, key, low, top_value):
    index_at = [jax.random.randint(jax.random.fold_in(key, axis), (), 0, length) for axis, length in enumerate(values.shape)]
    widest = values.shape.index(max(values.shape))
    neighbour = index_at[:widest] + [(index_at[widest] + 1) % values.shape[widest]] + index_at[widest + 1:]
    return values.at[tuple(index_at)].set(low).at[tuple(neighbour)].set(top_value)


def levels(own_key, extent, cuts, low, high):
    factor_of, own = 1.0, jax.random.fold_in(own_key, 6)
    for dim, blocks in cuts:
        steps = jnp.exp(jax.random.uniform(jax.random.fold_in(own, dim), (blocks,), jnp.float32, low / len(cuts), high / len(cuts)))
        factor_of = factor_of * jnp.repeat(steps, extent[dim] // blocks).reshape([-1 if axis == dim else 1 for axis in range(len(extent))])
    return factor_of


def normal_values(own_key, shape, deviation, most, shards=(), kind=jnp.bfloat16):
    gain = levels(own_key, shape, shards, -0.22, 0.18) if shards else 1.0
    values = jax.random.normal(own_key, shape, jnp.float32) * deviation * gain
    return jnp.minimum(jnp.maximum(values, -most), most).astype(kind)


def setup_inputs(seed: int = 0) -> dict:
    arg_keys = jax.random.split(jax.random.key(seed), 16)
    displacement = normal_values(arg_keys[0], (3, NODES), 1.0, 6.0, ((1, 128),), jnp.float32)
    disp_prev = normal_values(arg_keys[1], (3, NODES), 1.0, 6.0, ((1, 128),), jnp.float32)
    nodal_load = normal_values(arg_keys[2], (3, NODES), 1.0, 6.0, ((1, 128),), jnp.float32)
    nodal_mass = jnp.clip(jnp.exp(math.log(4.0) - 1.3862944 * jax.random.uniform(arg_keys[3], (NODES,), jnp.float32) ** levels(arg_keys[3], (NODES,), ((0, 128),), -0.2, 0.2)), 1.0, 4.0)
    modulus = jnp.clip(jnp.exp(math.log(10.0) - 2.3025851 * jax.random.uniform(arg_keys[4], (ELEMS,), jnp.float32) ** levels(arg_keys[4], (ELEMS,), ((0, 128),), -0.2, 0.2)), 1.0, 10.0)
    stiffness = draw_stiffness(jax.random.fold_in(arg_keys[15], 71), 0)
    connectivity = draw_connectivity(jax.random.fold_in(arg_keys[15], 71), 0)
    ghost_send = with_ends(jax.random.randint(arg_keys[7], (2, GHOSTS), 0, NODE_DEV), jax.random.fold_in(arg_keys[7], 1), 0, NODE_DEV - 1).astype(jnp.int32)
    contact_node = with_ends(jax.random.randint(arg_keys[8], (CONTACT,), 0, NODE_DEV), jax.random.fold_in(arg_keys[8], 1), 0, NODE_DEV - 1).astype(jnp.int32)
    contact_owner = draw_contact_owner(jax.random.fold_in(arg_keys[15], 71), 0)
    pair_ids = with_ends(jax.random.randint(arg_keys[10], (2, PAIRS), 0, 2 * CN_DEV), jax.random.fold_in(arg_keys[10], 1), 0, (2 * CN_DEV) - 1).astype(jnp.int32)
    gap_start = normal_values(arg_keys[11], (3, PAIRS), 0.5, 3.0, ((1, 128),), jnp.float32)
    penalty = jnp.clip(jnp.exp(math.log(2.0) - 1.3862944 * jax.random.uniform(arg_keys[12], (PAIRS,), jnp.float32) ** levels(arg_keys[12], (PAIRS,), ((0, 128),), -0.2, 0.2)), 0.5, 2.0)
    friction = jnp.clip(0.2 + 0.400000021 * jax.random.uniform(arg_keys[13], (PAIRS,), jnp.float32) ** levels(arg_keys[13], (PAIRS,), ((0, 128),), -0.2, 0.2), 0.2, 0.6)
    slip_state = with_ends((jax.random.randint(arg_keys[14], (STEPS, PAIRS), 0, 3) < 1).astype(jnp.int32), jax.random.fold_in(arg_keys[14], 1), 0, 1)
    return {"displacement": displacement, "disp_prev": disp_prev, "nodal_load": nodal_load, "nodal_mass": nodal_mass, "modulus": modulus, "stiffness": stiffness, "connectivity": connectivity, "ghost_send": ghost_send, "contact_node": contact_node, "contact_owner": contact_owner, "pair_ids": pair_ids, "gap_start": gap_start, "penalty": penalty, "friction": friction, "slip_state": slip_state}


time_step_sq = 0.05

def to_blocks(values, block_width):
    return values.reshape(values.shape[0], OWNER_TOTAL, block_width).transpose(1, 0, 2)

def from_blocks(values):
    return values.transpose(1, 0, 2).reshape(values.shape[1], -1)

def slot_rank(owners):
    onehot = (owners[:, None] == jnp.arange(OWNER_TOTAL, dtype=jnp.int32)[None, :]).astype(jnp.int32)
    earlier = jnp.cumsum(onehot, axis=0) - onehot
    return lax.optimization_barrier(jnp.sum(earlier * onehot, axis=1)).astype(jnp.int32)

def element_forces(extended, node_links, moduli, stiffness):
    gathered = extended[:, node_links].reshape(ELDOF, node_links.shape[1])
    product = jnp.dot(stiffness, gathered, precision=lax.Precision.HIGHEST) * moduli[None, :]
    return jnp.zeros_like(extended).at[:, node_links].add(product.reshape(3, ELNODE, node_links.shape[1]))

def contact_pair_forces(received_values, pair_ids, gap_start, penalty, friction, slipping):
    near_side = received_values[:, pair_ids[0]]
    far_side = received_values[:, pair_ids[1]]
    gap_vec = gap_start + far_side - near_side
    normal = penalty * jnp.maximum(-gap_vec[2], 0.0)
    tangent_gap = gap_vec[0:2]
    sticking = -0.5 * penalty[None, :] * tangent_gap
    length = jnp.sqrt(lax.optimization_barrier(jnp.sum(tangent_gap * tangent_gap, axis=0)) + 0.01)
    sliding = -friction[None, :] * normal[None, :] * tangent_gap / length[None, :]
    tangent = jnp.where(slipping[None, :] == 1, sliding, sticking)
    pair_force = jnp.concatenate([tangent, normal[None, :]], axis=0)
    result = jnp.zeros_like(received_values).at[:, pair_ids[1]].add(pair_force)
    return result.at[:, pair_ids[0]].add(-pair_force)

def lend_nodes(field_now, lend_ids):
    return field_now[:, lend_ids]

def add_ghosts(own_part, lend_ids, from_lower, from_upper):
    return own_part.at[:, lend_ids[0]].add(from_lower).at[:, lend_ids[1]].add(from_upper)

def fill_outbox(field_now, nodes, places):
    return jnp.zeros((3, OWNER_TOTAL * CAP), jnp.float32).at[:, places].set(field_now[:, nodes])

def take_back(returned, nodes, places):
    return jnp.zeros((3, NODE_DEV), jnp.float32).at[:, nodes].add(returned[:, places])

def one_device_forces(device_item, stiffness):
    return element_forces(device_item[0], device_item[1], device_item[2], stiffness)

def swap_owner(values):
    return values.reshape(OWNER_TOTAL, 3, OWNER_TOTAL, CAP).transpose(2, 1, 0, 3).reshape(OWNER_TOTAL, 3, OWNER_TOTAL * CAP)

def reference(displacement, disp_prev, nodal_load, nodal_mass, modulus, stiffness, connectivity, ghost_send, contact_node, contact_owner, pair_ids, gap_start, penalty, friction, slip_state):
    current = to_blocks(displacement, NODE_DEV)
    previous = to_blocks(disp_prev, NODE_DEV)
    loads = to_blocks(nodal_load, NODE_DEV)
    masses = nodal_mass.reshape(OWNER_TOTAL, 1, NODE_DEV)
    node_links = connectivity.reshape(ELNODE, OWNER_TOTAL, NE_DEV).transpose(1, 0, 2)
    moduli = modulus.reshape(OWNER_TOTAL, NE_DEV)
    lend_lists = ghost_send.reshape(2, OWNER_TOTAL, HB).transpose(1, 0, 2)
    contact_nodes = contact_node.reshape(OWNER_TOTAL, CN_DEV)
    contact_owners = contact_owner.reshape(OWNER_TOTAL, CN_DEV)
    places = contact_owners * CAP + jax.vmap(slot_rank)(contact_owners)
    contact_pair_lists = pair_ids.reshape(2, OWNER_TOTAL, PAIRS_PER_OWNER).transpose(1, 0, 2)
    gap_block_parts = to_blocks(gap_start, PAIRS_PER_OWNER)
    penalty_stiffnesses = penalty.reshape(OWNER_TOTAL, PAIRS_PER_OWNER)
    friction_coefficients = friction.reshape(OWNER_TOTAL, PAIRS_PER_OWNER)
    slip_flags = slip_state.reshape(STEPS, OWNER_TOTAL, PAIRS_PER_OWNER)
    blank_rim = jnp.zeros((1, 3, HB), jnp.float32)
    acceleration = current
    for tally_count in range(STEPS):
        outgoing = jax.vmap(lend_nodes)(current, lend_lists)
        lower_ghosts = jnp.concatenate([blank_rim, outgoing[:-1, :, 1]], axis=0)
        upper_ghosts = jnp.concatenate([outgoing[1:, :, 0], blank_rim], axis=0)
        extended = jnp.concatenate([current, lower_ghosts, upper_ghosts], axis=2)
        forces = lax.map(partial_forces(stiffness), (extended, node_links, moduli))
        from_upper = jnp.concatenate([forces[1:, :, NODE_DEV:NODE_DEV + HB], blank_rim], axis=0)
        from_lower = jnp.concatenate([blank_rim, forces[:-1, :, NODE_DEV + HB:]], axis=0)
        internal = jax.vmap(add_ghosts)(forces[:, :, :NODE_DEV], lend_lists, from_lower, from_upper)
        outboxes = jax.vmap(fill_outbox)(current, contact_nodes, places)
        received_values = swap_owner(outboxes)
        reply_messages = jax.vmap(contact_pair_forces)(received_values, contact_pair_lists, gap_block_parts, penalty_stiffnesses, friction_coefficients, slip_flags[tally_count])
        returned = swap_owner(reply_messages)
        contact = jax.vmap(take_back)(returned, contact_nodes, places)
        acceleration = (loads - internal + contact) / masses
        later = 2.0 * current - previous + time_step_sq * acceleration
        previous = current
        current = later
    return (from_blocks(current), from_blocks(acceleration))

def partial_forces(stiffness):

    def apply_one(device_item):
        return one_device_forces(device_item, stiffness)
    return apply_one
```

```python
import jax
import jax.numpy as jnp
from jax import lax
from jax.experimental import pallas as pl
from jax.experimental.pallas import tpu as pltpu
from jax.sharding import PartitionSpec as P

AXES = ("px", "py")
STEPS = 3
TIME_STEP_SQ = 0.05
LANES = 128
OWN = 32
EXT = 40
INNER = 384
f32, bf16, i32 = jnp.float32, jnp.bfloat16, jnp.int32


def iota_rows(rows, count):
    return lax.broadcasted_iota(i32, (rows, count), 0)


def split(x):
    head = x.astype(bf16)
    return head, (x - head.astype(f32)).astype(bf16)


def side_by_side(x):
    return jnp.concatenate(split(x), axis=1)


def one_hot(row):
    return jnp.where(iota_rows(LANES, row.shape[1]) == row, 1.0, 0.0).astype(bf16)


def pick(table, lo, hi, rows):
    hot = one_hot(lo)
    rows_of = jnp.dot(table, jnp.concatenate([hot, hot], axis=0), preferred_element_type=f32)
    mask = iota_rows(rows, lo.shape[1]) == hi
    return [
        jnp.where(mask, rows_of[c * rows : (c + 1) * rows], 0.0) for c in range(3)
    ]


def total(x):
    return jnp.sum(x, axis=0, keepdims=True)


def spread(values, lo, hi, rows):
    mask = iota_rows(rows, lo.shape[1]) == hi
    placed = jnp.concatenate([jnp.where(mask, v, 0.0) for v in values], axis=0).astype(bf16)
    return lax.dot_general(
        placed, one_hot(lo), (((1,), (1,)), ((), ())), preferred_element_type=f32
    )


def pieces(rows):
    heads = [r.astype(bf16).astype(f32) for r in rows]
    return heads + [r - h for r, h in zip(rows, heads)]


def joined(acc):
    half = acc.shape[0] // 2
    return acc[:half] + acc[half:]


def send_out(table, slots, lend, turned, outbox, to_lower, to_upper):
    both = side_by_side(table)
    turned[3 * OWN :, :] = jnp.zeros((LANES - 3 * OWN, LANES), f32)
    for r in range(0, OWN, 2):
        lo = jnp.concatenate([slots[r : r + 1, :], slots[r + 1 : r + 2, :]], axis=1)
        hi = jnp.concatenate([slots[OWN + r : OWN + r + 1, :], slots[OWN + r + 1 : OWN + r + 2, :]], axis=1)
        got = pick(both, lo, hi, OWN)
        for c in range(3):
            row = total(got[c])
            turned[c * OWN + r : c * OWN + r + 1, :] = row[:, :LANES]
            turned[c * OWN + r + 1 : c * OWN + r + 2, :] = row[:, LANES:]
    outbox[...] = turned[...].T
    for side, message in ((0, to_lower), (1, to_upper)):
        node = lend[side : side + 1, :]
        got = pick(both, node & 127, node >> 7, OWN)
        message[6:8, :] = jnp.zeros((2, LANES), f32)
        for c in range(3):
            row = total(got[c])
            message[2 * c : 2 * c + 1, :] = row[:, :LANES]
            message[2 * c + 1 : 2 * c + 2, :] = row[:, LANES:]


def begin_kernel(disp, prev, load, owner, node, lend, cur_o, prev_o, load_o, slots_o, outbox, to_lower, to_upper, turned):
    for src, dst in ((disp, cur_o), (prev, prev_o), (load, load_o)):
        for c in range(3):
            for h in range(OWN):
                dst[c * OWN + h : c * OWN + h + 1, :] = src[c : c + 1, h * LANES : (h + 1) * LANES]
    before = jnp.where(
        iota_rows(LANES, 2 * LANES) < lax.broadcasted_iota(i32, (LANES, 2 * LANES), 1), 1.0, 0.0
    ).astype(bf16)
    carry = jnp.zeros((LANES, LANES), f32)
    acc = jnp.zeros((2 * OWN, LANES), f32)
    for b in range(owner.shape[0]):
        hot = one_hot(owner[b : b + 1, :])
        counts = jnp.dot(hot, before, preferred_element_type=f32)
        earlier = carry + counts[:, :LANES]
        carry = carry + counts[:, LANES:]
        rank = total(jnp.where(hot.astype(f32) > 0.5, earlier, 0.0)).astype(i32)
        at = node[b : b + 1, :]
        mask = iota_rows(OWN, LANES) == rank
        put = jnp.concatenate(
            [
                jnp.where(mask, (at & 127).astype(f32), 0.0),
                jnp.where(mask, ((at >> 7) + 1).astype(f32), 0.0),
            ],
            axis=0,
        ).astype(bf16)
        acc = acc + lax.dot_general(put, hot, (((1,), (1,)), ((), ())), preferred_element_type=f32)
    found = acc.astype(i32)
    slots_o[:OWN, :] = found[:OWN]
    slots_o[OWN:, :] = found[OWN:] - 1
    send_out(cur_o[...], slots_o, lend, turned, outbox, to_lower, to_upper)


def element_loop(table, links, moduli, stiff, ue, fe, rows, first, count):
    nodes = links.shape[0]
    both = side_by_side(table)
    ue[...] = jnp.zeros(ue.shape, f32)
    cols = slice(first, first + count)

    for k in range(nodes):
        at = links[k : k + 1, cols]
        got = pick(both, at & 127, at >> 7, rows)
        for c in range(3):
            ue[c * OWN + k : c * OWN + k + 1, :] = total(got[c])
    u_head, u_tail = split(ue[...])
    k_head, k_tail = split(stiff[...])
    dot = lambda a, b: jnp.dot(a, b, preferred_element_type=f32)
    force = (dot(k_head, u_head) + dot(k_head, u_tail) + dot(k_tail, u_head)) * moduli[:, cols]
    head = force.astype(bf16).astype(f32)
    fe[: 3 * OWN, :] = head
    fe[3 * OWN :, :] = force - head

    acc = jnp.zeros((6 * rows, LANES), f32)
    for k in range(nodes):
        at = links[k : k + 1, cols]
        values = [fe[i * OWN + k : i * OWN + k + 1, :] for i in range(6)]
        acc = acc + spread(values, at & 127, at >> 7, rows)
    return joined(acc)


def inner_kernel(table, links, moduli, stiff, out, ue, fe):
    out[...] = element_loop(table[...], links, moduli, stiff, ue, fe, OWN, 0, INNER)


def rim_kernel(table, lower, upper, edge, links, moduli, stiff, out, back_lower, back_upper, ext, ue, fe):
    for c in range(3):
        ext[c * EXT : c * EXT + OWN, :] = table[c * OWN : (c + 1) * OWN, :]
        ext[c * EXT + OWN : c * EXT + OWN + 2, :] = lower[2 * c : 2 * c + 2, :] * edge[0:2, :]
        ext[c * EXT + OWN + 2 : c * EXT + OWN + 4, :] = upper[2 * c : 2 * c + 2, :] * edge[8:10, :]
        ext[c * EXT + OWN + 4 : (c + 1) * EXT, :] = jnp.zeros((EXT - OWN - 4, LANES), f32)
    ext[...] = element_loop(
        ext[...], links, moduli, stiff, ue, fe, EXT, INNER, links.shape[1] - INNER
    )
    back_lower[6:8, :] = jnp.zeros((2, LANES), f32)
    back_upper[6:8, :] = jnp.zeros((2, LANES), f32)
    for c in range(3):
        out[c * OWN : (c + 1) * OWN, :] = ext[c * EXT : c * EXT + OWN, :]
        back_lower[2 * c : 2 * c + 2, :] = ext[c * EXT + OWN : c * EXT + OWN + 2, :]
        back_upper[2 * c : 2 * c + 2, :] = ext[c * EXT + OWN + 2 : c * EXT + OWN + 4, :]


def pair_kernel(step, inbox, pairs, gap0, penalty, friction, slip, reply):
    both = side_by_side(inbox[...].T[: 3 * OWN])
    count = pairs.shape[1]
    wide = 256
    acc = jnp.zeros((6 * OWN, LANES), f32)
    for p in range(0, count, wide):
        cols = slice(p, p + wide)
        near, far = pairs[0:1, cols], pairs[1:2, cols]
        got_far = pick(both, far >> 5, far & 31, OWN)
        got_near = pick(both, near >> 5, near & 31, OWN)
        gap = [gap0[c : c + 1, cols] + total(got_far[c] - got_near[c]) for c in range(3)]
        stiff = penalty[:, cols]
        normal = stiff * jnp.maximum(-gap[2], 0.0)
        length = jnp.sqrt(gap[0] * gap[0] + gap[1] * gap[1] + 0.01)
        slide = -friction[:, cols] * normal / length
        factor = jnp.where(slip[step : step + 1, cols] == 1, slide, -0.5 * stiff)
        force = pieces([factor * gap[0], factor * gap[1], normal])
        acc = acc + spread(force, far >> 5, far & 31, OWN)
        acc = acc + spread([-v for v in force], near >> 5, near & 31, OWN)
    full = jnp.concatenate([joined(acc), jnp.zeros((LANES - 3 * OWN, LANES), f32)], axis=0)
    reply[...] = full.T


def new_state(cur, prev, load, mass, inner, rim, returned, from_lower, from_upper, edge, slots, lend, turned):
    turned[...] = returned[...].T
    acc = jnp.zeros((6 * OWN, LANES), f32)
    for r in range(0, OWN, 2):
        lo = jnp.concatenate([slots[r : r + 1, :], slots[r + 1 : r + 2, :]], axis=1)
        hi = jnp.concatenate([slots[OWN + r : OWN + r + 1, :], slots[OWN + r + 1 : OWN + r + 2, :]], axis=1)
        rows = [
            jnp.concatenate([turned[c * OWN + r : c * OWN + r + 1, :], turned[c * OWN + r + 1 : c * OWN + r + 2, :]], axis=1)
            for c in range(3)
        ]
        acc = acc + spread(pieces(rows), lo, hi, OWN)
    for side, message in ((0, from_lower), (1, from_upper)):
        node = lend[side : side + 1, :]
        here = -edge[8 * side : 8 * side + 1, :]
        rows = [
            jnp.concatenate([message[2 * c : 2 * c + 1, :] * here, message[2 * c + 1 : 2 * c + 2, :] * here], axis=1)
            for c in range(3)
        ]
        acc = acc + spread(pieces(rows), node & 127, node >> 7, OWN)
    force = load[...] - inner[...] - rim[...] + joined(acc)
    weight = mass[...]
    acceleration = force / jnp.concatenate([weight, weight, weight], axis=0)
    return 2.0 * cur[...] - prev[...] + TIME_STEP_SQ * acceleration, acceleration


def update_kernel(cur, prev, load, mass, inner, rim, returned, from_lower, from_upper, edge, slots, lend, cur_o, outbox, to_lower, to_upper, turned):
    later, _ = new_state(cur, prev, load, mass, inner, rim, returned, from_lower, from_upper, edge, slots, lend, turned)
    cur_o[...] = later
    send_out(later, slots, lend, turned, outbox, to_lower, to_upper)


def last_kernel(cur, prev, load, mass, inner, rim, returned, from_lower, from_upper, edge, slots, lend, disp_o, acc_o, turned, held):
    later, acceleration = new_state(
        cur, prev, load, mass, inner, rim, returned, from_lower, from_upper, edge, slots, lend, turned
    )
    for value, out in ((later, disp_o), (acceleration, acc_o)):
        held[...] = value
        for c in range(3):
            for h in range(OWN):
                out[c : c + 1, h * LANES : (h + 1) * LANES] = held[c * OWN + h : c * OWN + h + 1, :]


def call(kernel, outs, scratch, flops, *args):
    shapes = tuple(jax.ShapeDtypeStruct(s, t) for s, t in outs)
    space = pl.BlockSpec(memory_space=pltpu.VMEM)
    return pl.pallas_call(
        kernel,
        out_shape=shapes,
        in_specs=[space] * len(args),
        out_specs=tuple(space for _ in shapes),
        scratch_shapes=[pltpu.VMEM(s, f32) for s in scratch],
        compiler_params=pltpu.CompilerParams(vmem_limit_bytes=32 * 2**20),
        cost_estimate=pl.CostEstimate(flops=flops, bytes_accessed=2**20, transcendentals=0),
    )(*args)


def on_device(
    displacement,
    disp_prev,
    nodal_load,
    nodal_mass,
    modulus,
    stiffness,
    connectivity,
    ghost_send,
    contact_node,
    contact_owner,
    pair_ids,
    gap_start,
    penalty,
    friction,
    slip_state,
):
    devices = lax.axis_size(AXES)
    me = lax.axis_index(AXES)
    up = [(i, (i + 1) % devices) for i in range(devices)]
    down = [(j, i) for i, j in up]
    nodes = connectivity.shape[0]
    edge = jnp.broadcast_to(
        jnp.stack([me > 0, me < devices - 1]).astype(f32)[:, None, None], (2, 8, LANES)
    ).reshape(16, LANES)
    stiff = jnp.pad(
        stiffness.reshape(3, nodes, 3, nodes), ((0, 0), (0, OWN - nodes), (0, 0), (0, OWN - nodes))
    ).reshape(3 * OWN, 3 * OWN)
    mass = nodal_mass.reshape(OWN, LANES)
    moduli = modulus.reshape(1, -1)
    stiff_pair, rub = penalty.reshape(1, -1), friction.reshape(1, -1)
    owner, node = contact_owner.reshape(-1, LANES), contact_node.reshape(-1, LANES)
    table, message, square = ((3 * OWN, LANES), f32), ((8, LANES), f32), ((LANES, LANES), f32)
    turned = (LANES, LANES)

    def swap(x):
        return lax.all_to_all(x, AXES, split_axis=0, concat_axis=0, tiled=True)

    cur, prev, load, slots, outbox, to_lower, to_upper = call(
        begin_kernel,
        (table, table, table, ((2 * OWN, LANES), i32), square, message, message),
        (turned,),
        10**9,
        displacement, disp_prev, nodal_load, owner, node, ghost_send,
    )
    for step in range(STEPS):
        lower = lax.ppermute(to_upper, AXES, up)
        upper = lax.ppermute(to_lower, AXES, down)
        inbox = swap(outbox)
        (inner,) = call(
            inner_kernel,
            (table,),
            ((3 * OWN, INNER), (6 * OWN, INNER)),
            4 * 10**9,
            cur, connectivity, moduli, stiff,
        )
        rim, back_lower, back_upper = call(
            rim_kernel,
            (table, message, message),
            ((3 * EXT, LANES), (3 * OWN, connectivity.shape[1] - INNER), (6 * OWN, connectivity.shape[1] - INNER)),
            2 * 10**9,
            cur, lower, upper, edge, connectivity, moduli, stiff,
        )
        from_lower = lax.ppermute(back_upper, AXES, up)
        from_upper = lax.ppermute(back_lower, AXES, down)
        (reply,) = call(
            lambda *refs, step=step: pair_kernel(step, *refs),
            (square,),
            (),
            10**9,
            inbox, pair_ids, gap_start, stiff_pair, rub, slip_state,
        )
        returned = swap(reply)
        state = (cur, prev, load, mass, inner, rim, returned, from_lower, from_upper, edge, slots, ghost_send)
        if step < STEPS - 1:
            later, outbox, to_lower, to_upper = call(
                update_kernel, (table, square, message, message), (turned,), 10**9, *state
            )
            prev, cur = cur, later
        else:
            whole = (displacement.shape, f32)
            return call(last_kernel, (whole, whole), (turned, table[0]), 10**9, *state)


def solution(mesh):
    row, flat = P(None, AXES), P(AXES)
    return jax.shard_map(
        on_device,
        mesh=mesh,
        in_specs=(row, row, row, flat, flat, P(), row, row, flat, flat, row, row, flat, flat, row),
        out_specs=(row, row),
        check_vma=False,
    )
```

```python
import jax
import jax.numpy as jnp
from jax import lax
from jax.experimental import pallas as pl
from jax.experimental.pallas import tpu as pltpu
from jax.sharding import PartitionSpec as P

AXES = ("px", "py")
STEPS = 3
TIME_STEP_SQ = 0.05
LANES = 128
OWN = 32
GHOST = 16
SLOTS = 8
WIDE = 1024
INNER = 384
COST, LONG = 10**6, 10**9
f32, bf16, i32 = jnp.float32, jnp.bfloat16, jnp.int32


def iota_rows(rows, count):
    return lax.broadcasted_iota(i32, (rows, count), 0)


def split(x):
    head = x.astype(bf16)
    return head, (x - head.astype(f32)).astype(bf16)


def side_by_side(x):
    return jnp.concatenate(split(x), axis=1)


def matches(row, size):
    return iota_rows(size, row.shape[1]).astype(f32).astype(bf16) == row.astype(f32).astype(bf16)


def one_hot(row):
    return jnp.where(matches(row, LANES), jnp.ones((), bf16), jnp.zeros((), bf16))


def pick(table, lo, hi, rows):
    hot = one_hot(lo)
    rows_of = jnp.dot(table, jnp.concatenate([hot, hot], axis=0), preferred_element_type=f32)
    mask = iota_rows(rows, lo.shape[1]) == hi
    return [
        jnp.where(mask, rows_of[c * rows : (c + 1) * rows], 0.0) for c in range(3)
    ]


def total(x):
    return jnp.sum(x, axis=0, keepdims=True)


def spread(values, lo, hi, rows):
    mask = matches(hi, rows)
    zero = jnp.zeros((), bf16)
    placed = jnp.concatenate([jnp.where(mask, v.astype(bf16), zero) for v in values], axis=0)
    return lax.dot_general(
        placed, one_hot(lo), (((1,), (1,)), ((), ())), preferred_element_type=f32
    )


def pieces(rows):
    heads = [r.astype(bf16).astype(f32) for r in rows]
    return heads + [r - h for r, h in zip(rows, heads)]


def joined(acc):
    half = acc.shape[0] // 2
    return acc[:half] + acc[half:]


def beside(rows):
    return jnp.concatenate(rows, axis=1) if len(rows) > 1 else rows[0]


def slot_rows(slots, first):
    ranks = range(first, first + SLOTS)
    return beside([slots[r : r + 1, :] for r in ranks]), beside([slots[OWN + r : OWN + r + 1, :] for r in ranks])


def fill_outbox(table, slots, turned, outbox):
    both = side_by_side(table)
    turned[3 * OWN :, :] = jnp.zeros((LANES - 3 * OWN, LANES), f32)
    for first in range(0, OWN, SLOTS):
        lo, hi = slot_rows(slots, first)
        got = pick(both, lo, hi, OWN)
        for c in range(3):
            row = total(got[c])
            for i in range(SLOTS):
                at = c * OWN + first + i
                turned[at : at + 1, :] = row[:, i * LANES : (i + 1) * LANES]
    outbox[...] = turned[...].T


def odd():
    return lax.axis_index(AXES[1]) % 2 == 1


def by_parity(for_even, for_odd):
    return jnp.where(odd(), for_odd, for_even)


def fill_messages(table, lend, near, far):
    both = side_by_side(table)
    down, up = lend[0:1, :], lend[1:2, :]
    for node, message in ((by_parity(up, down), near), (by_parity(down, up), far)):
        got = pick(both, node & 127, node >> 7, OWN)
        message[6:8, :] = jnp.zeros((2, LANES), f32)
        for c in range(3):
            row = total(got[c])
            message[2 * c : 2 * c + 1, :] = row[:, :LANES]
            message[2 * c + 1 : 2 * c + 2, :] = row[:, LANES:]


def fold(src, dst):
    for c in range(3):
        for h in range(OWN):
            dst[c * OWN + h : c * OWN + h + 1, :] = src[c : c + 1, h * LANES : (h + 1) * LANES]


def begin_kernel(disp_hbm, owner_hbm, node_hbm, cur_o, slots_o, outbox, turned, disp, owner, node, sems):
    copies = [
        pltpu.make_async_copy(src, dst, sems.at[i])
        for i, (src, dst) in enumerate(((owner_hbm, owner), (node_hbm, node), (disp_hbm, disp)))
    ]
    for copy in copies:
        copy.start()
    before = jnp.where(
        iota_rows(LANES, 2 * LANES) < lax.broadcasted_iota(i32, (LANES, 2 * LANES), 1), 1.0, 0.0
    ).astype(bf16)
    copies[0].wait()
    copies[1].wait()
    blocks = owner.shape[0]
    hots = [one_hot(owner[b : b + 1, :]) for b in range(blocks)]
    counts = jnp.dot(jnp.concatenate(hots, axis=0), before, preferred_element_type=f32)
    carry = jnp.zeros((LANES, LANES), f32)
    ranks = []
    for b in range(blocks):
        here = counts[b * LANES : (b + 1) * LANES]
        mine = iota_rows(LANES, LANES) == owner[b : b + 1, :]
        ranks.append(total(jnp.where(mine, carry + here[:, :LANES], 0.0)))
        carry = carry + here[:, LANES:]
    at = beside([node[b : b + 1, :] for b in range(blocks)])
    mask = matches(beside(ranks).astype(i32), OWN)
    zero = jnp.zeros((), bf16)
    put = jnp.concatenate(
        [jnp.where(mask, v.astype(f32).astype(bf16), zero) for v in (at & 127, (at >> 7) + 1)], axis=0
    )
    acc = lax.dot_general(put, beside(hots), (((1,), (1,)), ((), ())), preferred_element_type=f32)
    found = acc.astype(i32)
    slots_o[:OWN, :] = found[:OWN]
    slots_o[OWN:, :] = found[OWN:] - 1
    copies[2].wait()
    fold(disp, cur_o)
    fill_outbox(cur_o[...], slots_o, turned, outbox)


def groups(nodes, size):
    return [range(k, min(k + size, nodes)) for k in range(0, nodes, size)]


def element_fields(table, links, ue, rows, low, first, count, size):
    nodes = links.shape[0]
    both = side_by_side(table)
    cols = slice(first, first + count)
    for group in groups(nodes, size):
        at = beside([links[k : k + 1, cols] for k in group])
        got = pick(both, at & 127, (at >> 7) - low, rows)
        for c in range(3):
            row = total(got[c])
            for i, k in enumerate(group):
                ue[c * nodes + k : c * nodes + k + 1, :] = row[:, i * count : (i + 1) * count]


def stiff_times(stiff, ue):
    u_head, u_tail = split(ue[...])
    k_head, k_tail = split(stiff[...])
    dot = lambda a, b: jnp.dot(a, b, preferred_element_type=f32)
    return dot(k_head, u_head) + dot(k_head, u_tail) + dot(k_tail, u_head)


def put_pieces(force, fe):
    head = force.astype(bf16).astype(f32)
    fe[0] = head
    fe[1] = force - head


def element_sums(links, parts, rows, low, first, size):
    nodes = links.shape[0]
    cols = slice(first, first + sum(fe.shape[2] for fe in parts))
    acc = jnp.zeros((6 * rows, LANES), f32)
    for group in groups(nodes, size):
        at = beside([links[k : k + 1, cols] for k in group])
        values = [
            beside([fe[i, c * nodes + k : c * nodes + k + 1, :] for k in group for fe in parts])
            for i in range(2)
            for c in range(3)
        ]
        acc = acc + spread(values, at & 127, (at >> 7) - low, rows)
    return joined(acc)


def lend_kernel(table, lend, near, far):
    fill_messages(table[...], lend, near, far)


def rim_own_kernel(table, links, stiff, out, ue):
    count = links.shape[1] - INNER
    element_fields(table[...], links, ue, OWN, 0, INNER, count, 8)
    out[...] = stiff_times(stiff, ue)


def edges():
    me = lax.axis_index(AXES[0]) * lax.axis_size(AXES[1]) + lax.axis_index(AXES[1])
    last = lax.axis_size(AXES[0]) * lax.axis_size(AXES[1]) - 1
    return jnp.where(me > 0, 1.0, 0.0), jnp.where(me < last, 1.0, 0.0)


def rim_kernel(_, own, far, near, links, moduli, stiff, fe, back_far, back_near, ext, ue):
    low, high = edges()
    count = links.shape[1] - INNER
    lower, upper = by_parity(far[...], near[...]) * low, by_parity(near[...], far[...]) * high
    ext[...] = jnp.zeros(ext.shape, f32)
    for c in range(3):
        ext[c * GHOST : c * GHOST + 2, :] = lower[2 * c : 2 * c + 2, :]
        ext[c * GHOST + 2 : c * GHOST + 4, :] = upper[2 * c : 2 * c + 2, :]
    element_fields(ext[...], links, ue, GHOST, OWN, INNER, count, 8)
    put_pieces((own[...] + stiff_times(stiff, ue)) * moduli[:, INNER:], fe)
    ext[...] = element_sums(links, [fe], GHOST, OWN, INNER, 8)
    pad = jnp.zeros((2, LANES), f32)
    below = jnp.concatenate([ext[c * GHOST : c * GHOST + 2, :] for c in range(3)] + [pad], axis=0)
    above = jnp.concatenate([ext[c * GHOST + 2 : c * GHOST + 4, :] for c in range(3)] + [pad], axis=0)
    back_near[...] = by_parity(above, below)
    back_far[...] = by_parity(below, above)


def inner_kernel(rim_fe, table, links, moduli, stiff, out, ue, fe):
    element_fields(table[...], links, ue, OWN, 0, 0, INNER, 2)
    put_pieces(stiff_times(stiff, ue) * moduli[:, :INNER], fe)
    out[...] = element_sums(links, [fe, rim_fe], OWN, 0, 0, 2)


def first_inner_kernel(rim_fe, table, links, moduli, stiff, prev, load, out, prev_o, load_o, ue, fe):
    inner_kernel(rim_fe, table, links, moduli, stiff, out, ue, fe)
    fold(prev, prev_o)
    fold(load, load_o)


def pair_kernel(step, _, __, inbox, pairs, gap0, penalty, friction, slip, reply):
    both = side_by_side(inbox[...].T[: 3 * OWN])
    count = pairs.shape[1]
    wide = WIDE
    acc = jnp.zeros((6 * OWN, LANES), f32)
    for p in range(0, count, wide):
        cols = slice(p, p + wide)
        near, far = pairs[0:1, cols], pairs[1:2, cols]
        got_far = pick(both, far >> 5, far & 31, OWN)
        got_near = pick(both, near >> 5, near & 31, OWN)
        gap = [gap0[c : c + 1, cols] + total(got_far[c] - got_near[c]) for c in range(3)]
        stiff = penalty[:, cols]
        normal = stiff * jnp.maximum(-gap[2], 0.0)
        length = jnp.sqrt(gap[0] * gap[0] + gap[1] * gap[1] + 0.01)
        slide = -friction[:, cols] * normal / length
        factor = jnp.where(slip[step : step + 1, cols] == 1, slide, -0.5 * stiff)
        force = pieces([factor * gap[0], factor * gap[1], normal])
        both_ends = beside([far, near])
        force = [beside([v, -v]) for v in force]
        acc = acc + spread(force, both_ends >> 5, both_ends & 31, OWN)
    full = jnp.concatenate([joined(acc), jnp.zeros((LANES - 3 * OWN, LANES), f32)], axis=0)
    reply[...] = full.T


def new_state(cur, prev, load, mass, inner, returned, far, near, slots, lend, turned):
    turned[...] = returned[...].T
    acc = jnp.zeros((6 * OWN, LANES), f32)
    for first in range(0, OWN, SLOTS):
        lo, hi = slot_rows(slots, first)
        rows = [
            beside([turned[c * OWN + r : c * OWN + r + 1, :] for r in range(first, first + SLOTS)])
            for c in range(3)
        ]
        acc = acc + spread(pieces(rows), lo, hi, OWN)
    near, far = near[...], far[...]
    for side, message in ((0, by_parity(far, near)), (1, by_parity(near, far))):
        node = lend[side : side + 1, :]
        here = -edges()[side]
        rows = [
            jnp.concatenate([message[2 * c : 2 * c + 1, :] * here, message[2 * c + 1 : 2 * c + 2, :] * here], axis=1)
            for c in range(3)
        ]
        acc = acc + spread(pieces(rows), node & 127, node >> 7, OWN)
    force = load[...] - inner[...] + joined(acc)
    weight = mass[...]
    acceleration = force / jnp.concatenate([weight, weight, weight], axis=0)
    return 2.0 * cur[...] - prev[...] + TIME_STEP_SQ * acceleration, acceleration


def update_kernel(cur, prev, load, mass, inner, returned, far, near, slots, lend, cur_o, outbox, turned):
    later, _ = new_state(cur, prev, load, mass, inner, returned, far, near, slots, lend, turned)
    cur_o[...] = later
    fill_outbox(later, slots, turned, outbox)


def last_kernel(cur, prev, load, mass, inner, returned, far, near, slots, lend, disp_o, acc_o, turned, held):
    later, acceleration = new_state(
        cur, prev, load, mass, inner, returned, far, near, slots, lend, turned
    )
    for value, out in ((later, disp_o), (acceleration, acc_o)):
        held[...] = value
        for c in range(3):
            for h in range(OWN):
                out[c : c + 1, h * LANES : (h + 1) * LANES] = held[c * OWN + h : c * OWN + h + 1, :]


def call(kernel, outs, scratch, flops, *args, outside=(), hbm=()):
    shapes = tuple(jax.ShapeDtypeStruct(s, t) for s, t in outs)
    space, anywhere = pl.BlockSpec(memory_space=pltpu.VMEM), pl.BlockSpec(memory_space=pl.ANY)
    far_off = pl.BlockSpec(memory_space=pltpu.HBM)
    return pl.pallas_call(
        kernel,
        out_shape=shapes,
        in_specs=[far_off if i in hbm else anywhere if i in outside else space for i in range(len(args))],
        out_specs=tuple(space for _ in shapes),
        scratch_shapes=[pltpu.VMEM(s, f32) if isinstance(s, tuple) else s for s in scratch],
        compiler_params=pltpu.CompilerParams(vmem_limit_bytes=32 * 2**20),
        cost_estimate=pl.CostEstimate(flops=flops, bytes_accessed=2**20, transcendentals=0),
    )(*args)


def on_device(
    displacement,
    disp_prev,
    nodal_load,
    nodal_mass,
    modulus,
    stiffness,
    connectivity,
    ghost_send,
    contact_node,
    contact_owner,
    pair_ids,
    gap_start,
    penalty,
    friction,
    slip_state,
):
    devices = lax.axis_size(AXES)
    near_pairs = [(i, i ^ 1) for i in range(devices)]
    far_pairs = [(i, (i + 2 * (i % 2) - 1) % devices) for i in range(devices)]
    nodes = connectivity.shape[0]
    mass = nodal_mass.reshape(OWN, LANES)
    moduli = modulus.reshape(1, -1)
    stiff_pair, rub = penalty.reshape(1, -1), friction.reshape(1, -1)
    owner, node = contact_owner.reshape(-1, LANES), contact_node.reshape(-1, LANES)
    table, message, square = ((3 * OWN, LANES), f32), ((8, LANES), f32), ((LANES, LANES), f32)
    turned = (LANES, LANES)

    def swap(x):
        return lax.all_to_all(x, AXES, split_axis=0, concat_axis=0, tiled=True)

    cur, slots, outbox = call(
        begin_kernel,
        (table, ((2 * OWN, LANES), i32), square),
        (
            turned,
            displacement.shape,
            pltpu.VMEM(owner.shape, i32),
            pltpu.VMEM(node.shape, i32),
            pltpu.SemaphoreType.DMA((3,)),
        ),
        COST,
        displacement, owner, node,
        hbm=(0, 1, 2),
    )
    prev = load = None
    rim_count = connectivity.shape[1] - INNER
    rows = connectivity.shape[0] * 3
    for step in range(STEPS):
        inbox = swap(outbox)
        near, far = call(lend_kernel, (message, message), (), LONG, cur, ghost_send)
        lent = near
        near = lax.ppermute(near, AXES, near_pairs)
        far = lax.ppermute(far, AXES, far_pairs)
        (rim_own,) = call(
            rim_own_kernel,
            (((rows, rim_count), f32),),
            ((rows, rim_count),),
            LONG,
            cur, connectivity, stiffness,
        )
        (reply,) = call(
            lambda *refs, step=step: pair_kernel(step, *refs),
            (square,),
            (),
            LONG,
            lent, rim_own, inbox, pair_ids, gap_start, stiff_pair, rub, slip_state,
            outside=(0, 1),
        )
        rim, far, near = call(
            rim_kernel,
            (((2, rows, rim_count), f32), message, message),
            ((3 * GHOST, LANES), (rows, rim_count)),
            LONG,
            reply, rim_own, far, near, connectivity, moduli, stiffness,
            outside=(0,),
        )
        far = lax.ppermute(far, AXES, far_pairs)
        near = lax.ppermute(near, AXES, near_pairs)
        inner_scratch = ((rows, INNER), (2, rows, INNER))
        inner_args = (rim, cur, connectivity, moduli, stiffness)
        if step == 0:
            inner, prev, load = call(
                first_inner_kernel,
                (table, table, table),
                inner_scratch,
                COST,
                *inner_args, disp_prev, nodal_load,
            )
        else:
            (inner,) = call(inner_kernel, (table,), inner_scratch, COST, *inner_args)
        returned = swap(reply)
        state = (cur, prev, load, mass, inner, returned, far, near, slots, ghost_send)
        if step < STEPS - 1:
            later, outbox = call(update_kernel, (table, square), (turned,), COST, *state)
            prev, cur = cur, later
        else:
            whole = (displacement.shape, f32)
            return call(last_kernel, (whole, whole), (turned, table[0]), COST, *state)


def solution(mesh):
    row, flat = P(None, AXES), P(AXES)
    return jax.shard_map(
        on_device,
        mesh=mesh,
        in_specs=(row, row, row, flat, flat, P(), row, row, flat, flat, row, row, flat, flat, row),
        out_specs=(row, row),
        check_vma=False,
    )
```

```python
import jax
import jax.numpy as jnp
from jax import lax
from jax.experimental import pallas as pl
from jax.experimental.pallas import tpu as pltpu
from jax.sharding import PartitionSpec as P

AXES = ("px", "py")
STEPS = 3
TIME_STEP_SQ = 0.05
LANES = 128
OWN = 32
GHOST = 16
SLOTS = 8
WIDE = 1024
INNER = 384
COST, LONG = 10**6, 10**9
f32, bf16, i32 = jnp.float32, jnp.bfloat16, jnp.int32


def iota_rows(rows, count):
    return lax.broadcasted_iota(i32, (rows, count), 0)


def split(x):
    head = x.astype(bf16)
    return head, (x - head.astype(f32)).astype(bf16)


def side_by_side(x):
    return jnp.concatenate(split(x), axis=1)


def matches(row, size):
    return iota_rows(size, row.shape[1]).astype(f32).astype(bf16) == row.astype(f32).astype(bf16)


def one_hot(row):
    return jnp.where(matches(row, LANES), jnp.ones((), bf16), jnp.zeros((), bf16))


def pick(table, lo, hi, rows):
    hot = one_hot(lo)
    rows_of = jnp.dot(table, jnp.concatenate([hot, hot], axis=0), preferred_element_type=f32)
    mask = iota_rows(rows, lo.shape[1]) == hi
    return [
        jnp.where(mask, rows_of[c * rows : (c + 1) * rows], 0.0) for c in range(3)
    ]


def pick_few(table, lo, hi, rows):
    rows_of = joined(jnp.dot(table, one_hot(lo), preferred_element_type=f32))
    mask = iota_rows(rows, lo.shape[1]) == hi
    return [
        jnp.where(mask, rows_of[c * rows : (c + 1) * rows], 0.0) for c in range(3)
    ]


def total(x):
    return jnp.sum(x, axis=0, keepdims=True)


def spread(values, lo, hi, rows):
    mask = matches(hi, rows)
    zero = jnp.zeros((), bf16)
    placed = jnp.concatenate([jnp.where(mask, v.astype(bf16), zero) for v in values], axis=0)
    return lax.dot_general(
        placed, one_hot(lo), (((1,), (1,)), ((), ())), preferred_element_type=f32
    )


def pieces(rows):
    heads = [r.astype(bf16).astype(f32) for r in rows]
    return heads + [r - h for r, h in zip(rows, heads)]


def joined(acc):
    half = acc.shape[0] // 2
    return acc[:half] + acc[half:]


def beside(rows):
    return jnp.concatenate(rows, axis=1) if len(rows) > 1 else rows[0]


def slot_rows(slots, first):
    ranks = range(first, first + SLOTS)
    return beside([slots[r : r + 1, :] for r in ranks]), beside([slots[OWN + r : OWN + r + 1, :] for r in ranks])


def fill_outbox(table, slots, turned, outbox):
    both = side_by_side(table)
    turned[3 * OWN :, :] = jnp.zeros((LANES - 3 * OWN, LANES), f32)
    for first in range(0, OWN, SLOTS):
        lo, hi = slot_rows(slots, first)
        got = pick(both, lo, hi, OWN)
        for c in range(3):
            row = total(got[c])
            for i in range(SLOTS):
                at = c * OWN + first + i
                turned[at : at + 1, :] = row[:, i * LANES : (i + 1) * LANES]
    outbox[...] = turned[...].T


def odd():
    return lax.axis_index(AXES[1]) % 2 == 1


def by_parity(for_even, for_odd):
    return jnp.where(odd(), for_odd, for_even)


def fill_messages(table, lend, near, far):
    both = side_by_side(table)
    down, up = lend[0:1, :], lend[1:2, :]
    for node, message in ((by_parity(up, down), near), (by_parity(down, up), far)):
        got = pick(both, node & 127, node >> 7, OWN)
        message[6:8, :] = jnp.zeros((2, LANES), f32)
        for c in range(3):
            row = total(got[c])
            message[2 * c : 2 * c + 1, :] = row[:, :LANES]
            message[2 * c + 1 : 2 * c + 2, :] = row[:, LANES:]


def fold(src, dst):
    for c in range(3):
        for h in range(OWN):
            dst[c * OWN + h : c * OWN + h + 1, :] = src[c : c + 1, h * LANES : (h + 1) * LANES]


def begin_kernel(disp_hbm, owner_hbm, node_hbm, cur_o, slots_o, outbox, turned, disp, owner, node, sems):
    copies = [
        pltpu.make_async_copy(src, dst, sems.at[i])
        for i, (src, dst) in enumerate(((owner_hbm, owner), (node_hbm, node), (disp_hbm, disp)))
    ]
    for copy in copies:
        copy.start()
    before = jnp.where(
        iota_rows(LANES, 2 * LANES) < lax.broadcasted_iota(i32, (LANES, 2 * LANES), 1), 1.0, 0.0
    ).astype(bf16)
    copies[0].wait()
    copies[1].wait()
    blocks = owner.shape[0]
    hots = [one_hot(owner[b : b + 1, :]) for b in range(blocks)]
    counts = jnp.dot(jnp.concatenate(hots, axis=0), before, preferred_element_type=f32)
    carry = jnp.zeros((LANES, LANES), f32)
    ranks = []
    for b in range(blocks):
        here = counts[b * LANES : (b + 1) * LANES]
        mine = iota_rows(LANES, LANES) == owner[b : b + 1, :]
        ranks.append(total(jnp.where(mine, carry + here[:, :LANES], 0.0)))
        carry = carry + here[:, LANES:]
    at = beside([node[b : b + 1, :] for b in range(blocks)])
    mask = matches(beside(ranks).astype(i32), OWN)
    zero = jnp.zeros((), bf16)
    put = jnp.concatenate(
        [jnp.where(mask, v.astype(f32).astype(bf16), zero) for v in (at & 127, (at >> 7) + 1)], axis=0
    )
    acc = lax.dot_general(put, beside(hots), (((1,), (1,)), ((), ())), preferred_element_type=f32)
    found = acc.astype(i32)
    slots_o[:OWN, :] = found[:OWN]
    slots_o[OWN:, :] = found[OWN:] - 1
    copies[2].wait()
    fold(disp, cur_o)
    fill_outbox(cur_o[...], slots_o, turned, outbox)


def groups(nodes, size):
    return [range(k, min(k + size, nodes)) for k in range(0, nodes, size)]


def element_fields(table, links, ue, rows, low, first, count, size):
    nodes = links.shape[0]
    few = rows < OWN
    both = jnp.concatenate(split(table), axis=0) if few else side_by_side(table)
    cols = slice(first, first + count)
    for group in groups(nodes, size):
        at = beside([links[k : k + 1, cols] for k in group])
        got = (pick_few if few else pick)(both, at & 127, (at >> 7) - low, rows)
        for c in range(3):
            row = total(got[c])
            for i, k in enumerate(group):
                ue[c * nodes + k : c * nodes + k + 1, :] = row[:, i * count : (i + 1) * count]


def stiff_times(stiff, ue):
    u_head, u_tail = split(ue[...])
    k_head, k_tail = split(stiff[...])
    dot = lambda a, b: jnp.dot(a, b, preferred_element_type=f32)
    twice = dot(k_head, beside([u_head, u_tail]))
    count = ue.shape[1]
    return twice[:, :count] + twice[:, count:] + dot(k_tail, u_head)


def put_pieces(force, fe):
    head = force.astype(bf16).astype(f32)
    fe[0] = head
    fe[1] = force - head


def element_sums(links, parts, rows, low, first, size):
    nodes = links.shape[0]
    cols = slice(first, first + sum(fe.shape[2] for fe in parts))
    acc = jnp.zeros((6 * rows, LANES), f32)
    for group in groups(nodes, size):
        at = beside([links[k : k + 1, cols] for k in group])
        values = [
            beside([fe[i, c * nodes + k : c * nodes + k + 1, :] for k in group for fe in parts])
            for i in range(2)
            for c in range(3)
        ]
        acc = acc + spread(values, at & 127, (at >> 7) - low, rows)
    return joined(acc)


def lend_kernel(table, lend, near, far):
    fill_messages(table[...], lend, near, far)


def rim_own_kernel(table, links, stiff, out, ue):
    count = links.shape[1] - INNER
    element_fields(table[...], links, ue, OWN, 0, INNER, count, 8)
    out[...] = stiff_times(stiff, ue)


def edges():
    me = lax.axis_index(AXES[0]) * lax.axis_size(AXES[1]) + lax.axis_index(AXES[1])
    last = lax.axis_size(AXES[0]) * lax.axis_size(AXES[1]) - 1
    return jnp.where(me > 0, 1.0, 0.0), jnp.where(me < last, 1.0, 0.0)


def rim_kernel(_, own, far, near, links, moduli, stiff, fe, back_far, back_near, ext, ue):
    low, high = edges()
    count = links.shape[1] - INNER
    lower, upper = by_parity(far[...], near[...]) * low, by_parity(near[...], far[...]) * high
    ext[...] = jnp.zeros(ext.shape, f32)
    for c in range(3):
        ext[c * GHOST : c * GHOST + 2, :] = lower[2 * c : 2 * c + 2, :]
        ext[c * GHOST + 2 : c * GHOST + 4, :] = upper[2 * c : 2 * c + 2, :]
    element_fields(ext[...], links, ue, GHOST, OWN, INNER, count, 8)
    put_pieces((own[...] + stiff_times(stiff, ue)) * moduli[:, INNER:], fe)
    ext[...] = element_sums(links, [fe], GHOST, OWN, INNER, 8)
    pad = jnp.zeros((2, LANES), f32)
    below = jnp.concatenate([ext[c * GHOST : c * GHOST + 2, :] for c in range(3)] + [pad], axis=0)
    above = jnp.concatenate([ext[c * GHOST + 2 : c * GHOST + 4, :] for c in range(3)] + [pad], axis=0)
    back_near[...] = by_parity(above, below)
    back_far[...] = by_parity(below, above)


def inner_kernel(rim_fe, table, links, moduli, stiff, out, ue, fe):
    element_fields(table[...], links, ue, OWN, 0, 0, INNER, 2)
    put_pieces(stiff_times(stiff, ue) * moduli[:, :INNER], fe)
    out[...] = element_sums(links, [fe, rim_fe], OWN, 0, 0, 2)


def first_inner_kernel(rim_fe, table, links, moduli, stiff, prev, load, out, prev_o, load_o, ue, fe):
    inner_kernel(rim_fe, table, links, moduli, stiff, out, ue, fe)
    fold(prev, prev_o)
    fold(load, load_o)


def pair_kernel(step, _, __, inbox, pairs, gap0, penalty, friction, slip, reply):
    both = side_by_side(inbox[...].T[: 3 * OWN])
    count = pairs.shape[1]
    wide = WIDE
    acc = jnp.zeros((6 * OWN, LANES), f32)
    for p in range(0, count, wide):
        cols = slice(p, p + wide)
        near, far = pairs[0:1, cols], pairs[1:2, cols]
        got_far = pick(both, far >> 5, far & 31, OWN)
        got_near = pick(both, near >> 5, near & 31, OWN)
        gap = [gap0[c : c + 1, cols] + total(got_far[c] - got_near[c]) for c in range(3)]
        stiff = penalty[:, cols]
        normal = stiff * jnp.maximum(-gap[2], 0.0)
        length = jnp.sqrt(gap[0] * gap[0] + gap[1] * gap[1] + 0.01)
        slide = -friction[:, cols] * normal / length
        factor = jnp.where(slip[step : step + 1, cols] == 1, slide, -0.5 * stiff)
        force = pieces([factor * gap[0], factor * gap[1], normal])
        both_ends = beside([far, near])
        force = [beside([v, -v]) for v in force]
        acc = acc + spread(force, both_ends >> 5, both_ends & 31, OWN)
    full = jnp.concatenate([joined(acc), jnp.zeros((LANES - 3 * OWN, LANES), f32)], axis=0)
    reply[...] = full.T


def new_state(cur, prev, load, mass, inner, returned, far, near, slots, lend, turned):
    turned[...] = returned[...].T
    acc = jnp.zeros((6 * OWN, LANES), f32)
    for first in range(0, OWN, SLOTS):
        lo, hi = slot_rows(slots, first)
        rows = [
            beside([turned[c * OWN + r : c * OWN + r + 1, :] for r in range(first, first + SLOTS)])
            for c in range(3)
        ]
        acc = acc + spread(pieces(rows), lo, hi, OWN)
    near, far = near[...], far[...]
    for side, message in ((0, by_parity(far, near)), (1, by_parity(near, far))):
        node = lend[side : side + 1, :]
        here = -edges()[side]
        rows = [
            jnp.concatenate([message[2 * c : 2 * c + 1, :] * here, message[2 * c + 1 : 2 * c + 2, :] * here], axis=1)
            for c in range(3)
        ]
        acc = acc + spread(pieces(rows), node & 127, node >> 7, OWN)
    force = load[...] - inner[...] + joined(acc)
    weight = mass[...]
    acceleration = force / jnp.concatenate([weight, weight, weight], axis=0)
    return 2.0 * cur[...] - prev[...] + TIME_STEP_SQ * acceleration, acceleration


def update_kernel(cur, prev, load, mass, inner, returned, far, near, slots, lend, cur_o, outbox, turned):
    later, _ = new_state(cur, prev, load, mass, inner, returned, far, near, slots, lend, turned)
    cur_o[...] = later
    fill_outbox(later, slots, turned, outbox)


def last_kernel(cur, prev, load, mass, inner, returned, far, near, slots, lend, disp_o, acc_o, turned, held):
    later, acceleration = new_state(
        cur, prev, load, mass, inner, returned, far, near, slots, lend, turned
    )
    for value, out in ((later, disp_o), (acceleration, acc_o)):
        held[...] = value
        for c in range(3):
            for h in range(OWN):
                out[c : c + 1, h * LANES : (h + 1) * LANES] = held[c * OWN + h : c * OWN + h + 1, :]


def call(kernel, outs, scratch, flops, *args, outside=(), hbm=(), vmem=32):
    shapes = tuple(jax.ShapeDtypeStruct(s, t) for s, t in outs)
    space, anywhere = pl.BlockSpec(memory_space=pltpu.VMEM), pl.BlockSpec(memory_space=pl.ANY)
    in_hbm = pl.BlockSpec(memory_space=pltpu.HBM)
    return pl.pallas_call(
        kernel,
        out_shape=shapes,
        in_specs=[in_hbm if i in hbm else anywhere if i in outside else space for i in range(len(args))],
        out_specs=tuple(space for _ in shapes),
        scratch_shapes=[pltpu.VMEM(s, f32) if isinstance(s, tuple) else s for s in scratch],
        compiler_params=pltpu.CompilerParams(vmem_limit_bytes=vmem * 2**20),
        cost_estimate=pl.CostEstimate(flops=flops, bytes_accessed=2**20, transcendentals=0),
    )(*args)


def on_device(
    displacement,
    disp_prev,
    nodal_load,
    nodal_mass,
    modulus,
    stiffness,
    connectivity,
    ghost_send,
    contact_node,
    contact_owner,
    pair_ids,
    gap_start,
    penalty,
    friction,
    slip_state,
):
    devices = lax.axis_size(AXES)
    near_pairs = [(i, i ^ 1) for i in range(devices)]
    far_pairs = [(i, (i + 2 * (i % 2) - 1) % devices) for i in range(devices)]
    nodes = connectivity.shape[0]
    mass = nodal_mass.reshape(OWN, LANES)
    moduli = modulus.reshape(1, -1)
    stiff_pair, rub = penalty.reshape(1, -1), friction.reshape(1, -1)
    owner, node = contact_owner.reshape(-1, LANES), contact_node.reshape(-1, LANES)
    table, message, square = ((3 * OWN, LANES), f32), ((8, LANES), f32), ((LANES, LANES), f32)
    turned = (LANES, LANES)

    def swap(x):
        return lax.all_to_all(x, AXES, split_axis=0, concat_axis=0, tiled=True)

    cur, slots, outbox = call(
        begin_kernel,
        (table, ((2 * OWN, LANES), i32), square),
        (
            turned,
            displacement.shape,
            pltpu.VMEM(owner.shape, i32),
            pltpu.VMEM(node.shape, i32),
            pltpu.SemaphoreType.DMA((3,)),
        ),
        COST,
        displacement, owner, node,
        hbm=(0, 1, 2),
        vmem=60,
    )
    prev = load = None
    rim_count = connectivity.shape[1] - INNER
    rows = connectivity.shape[0] * 3
    for step in range(STEPS):
        inbox = swap(outbox)
        near, far = call(lend_kernel, (message, message), (), LONG, cur, ghost_send)
        lent = near
        near = lax.ppermute(near, AXES, near_pairs)
        far = lax.ppermute(far, AXES, far_pairs)
        (rim_own,) = call(
            rim_own_kernel,
            (((rows, rim_count), f32),),
            ((rows, rim_count),),
            LONG,
            cur, connectivity, stiffness,
        )
        (reply,) = call(
            lambda *refs, step=step: pair_kernel(step, *refs),
            (square,),
            (),
            LONG,
            lent, rim_own, inbox, pair_ids, gap_start, stiff_pair, rub, slip_state,
            outside=(0, 1),
        )
        rim, far, near = call(
            rim_kernel,
            (((2, rows, rim_count), f32), message, message),
            ((3 * GHOST, LANES), (rows, rim_count)),
            LONG,
            reply, rim_own, far, near, connectivity, moduli, stiffness,
            outside=(0,),
        )
        far = lax.ppermute(far, AXES, far_pairs)
        near = lax.ppermute(near, AXES, near_pairs)
        inner_scratch = ((rows, INNER), (2, rows, INNER))
        inner_args = (rim, cur, connectivity, moduli, stiffness)
        if step == 0:
            inner, prev, load = call(
                first_inner_kernel,
                (table, table, table),
                inner_scratch,
                COST,
                *inner_args, disp_prev, nodal_load,
            )
        else:
            (inner,) = call(inner_kernel, (table,), inner_scratch, COST, *inner_args)
        returned = swap(reply)
        state = (cur, prev, load, mass, inner, returned, far, near, slots, ghost_send)
        if step < STEPS - 1:
            later, outbox = call(update_kernel, (table, square), (turned,), COST, *state)
            prev, cur = cur, later
        else:
            whole = (displacement.shape, f32)
            return call(last_kernel, (whole, whole), (turned, table[0]), COST, *state)


def solution(mesh):
    row, flat = P(None, AXES), P(AXES)
    return jax.shard_map(
        on_device,
        mesh=mesh,
        in_specs=(row, row, row, flat, flat, P(), row, row, flat, flat, row, row, flat, flat, row),
        out_specs=(row, row),
        check_vma=False,
    )
```

```python
import jax
import jax.numpy as jnp
from jax import lax
from jax.experimental import pallas as pl
from jax.experimental.pallas import tpu as pltpu
from jax.sharding import PartitionSpec as P

AXES = ("px", "py")
STEPS = 3
TIME_STEP_SQ = 0.05
LANES = 128
OWN = 32
GHOST = 16
SLOTS = 8
WIDE = 1024
INNER = 384
COST, LONG = 10**6, 10**9
f32, bf16, i32 = jnp.float32, jnp.bfloat16, jnp.int32


def iota_rows(rows, count):
    return lax.broadcasted_iota(i32, (rows, count), 0)


def split(x):
    head = x.astype(bf16)
    return head, (x - head.astype(f32)).astype(bf16)


def side_by_side(x):
    return jnp.concatenate(split(x), axis=1)


def matches(row, size):
    return iota_rows(size, row.shape[1]).astype(f32).astype(bf16) == row.astype(f32).astype(bf16)


def one_hot(row):
    return jnp.where(matches(row, LANES), jnp.ones((), bf16), jnp.zeros((), bf16))


def pick(table, lo, hi, rows):
    hot = one_hot(lo)
    rows_of = jnp.dot(table, jnp.concatenate([hot, hot], axis=0), preferred_element_type=f32)
    mask = iota_rows(rows, lo.shape[1]) == hi
    return [
        jnp.where(mask, rows_of[c * rows : (c + 1) * rows], 0.0) for c in range(3)
    ]


def pick_few(table, lo, hi, rows):
    rows_of = joined(jnp.dot(table, one_hot(lo), preferred_element_type=f32))
    mask = iota_rows(rows, lo.shape[1]) == hi
    return [
        jnp.where(mask, rows_of[c * rows : (c + 1) * rows], 0.0) for c in range(3)
    ]


def total(x):
    return jnp.sum(x, axis=0, keepdims=True)


def spread(values, lo, hi, rows):
    mask = matches(hi, rows)
    zero = jnp.zeros((), bf16)
    placed = jnp.concatenate([jnp.where(mask, v.astype(bf16), zero) for v in values], axis=0)
    return lax.dot_general(
        placed, one_hot(lo), (((1,), (1,)), ((), ())), preferred_element_type=f32
    )


def pieces(rows):
    heads = [r.astype(bf16).astype(f32) for r in rows]
    return heads + [r - h for r, h in zip(rows, heads)]


def joined(acc):
    half = acc.shape[0] // 2
    return acc[:half] + acc[half:]


def beside(rows):
    return jnp.concatenate(rows, axis=1) if len(rows) > 1 else rows[0]


def slot_rows(slots, first):
    ranks = range(first, first + SLOTS)
    return beside([slots[r : r + 1, :] for r in ranks]), beside([slots[OWN + r : OWN + r + 1, :] for r in ranks])


def fill_outbox(table, slots, turned, outbox):
    both = side_by_side(table)
    turned[3 * OWN :, :] = jnp.zeros((LANES - 3 * OWN, LANES), f32)
    for first in range(0, OWN, SLOTS):
        lo, hi = slot_rows(slots, first)
        got = pick(both, lo, hi, OWN)
        for c in range(3):
            row = total(got[c])
            for i in range(SLOTS):
                at = c * OWN + first + i
                turned[at : at + 1, :] = row[:, i * LANES : (i + 1) * LANES]
    outbox[...] = turned[...].T


def odd():
    return lax.axis_index(AXES[1]) % 2 == 1


def by_parity(for_even, for_odd):
    return jnp.where(odd(), for_odd, for_even)


def fill_messages(table, lend, near, far):
    both = side_by_side(table)
    down, up = lend[0:1, :], lend[1:2, :]
    for node, message in ((by_parity(up, down), near), (by_parity(down, up), far)):
        got = pick(both, node & 127, node >> 7, OWN)
        message[6:8, :] = jnp.zeros((2, LANES), f32)
        for c in range(3):
            row = total(got[c])
            message[2 * c : 2 * c + 1, :] = row[:, :LANES]
            message[2 * c + 1 : 2 * c + 2, :] = row[:, LANES:]


def fold(src, dst):
    for c in range(3):
        for h in range(OWN):
            dst[c * OWN + h : c * OWN + h + 1, :] = src[c : c + 1, h * LANES : (h + 1) * LANES]


def begin_kernel(disp_hbm, owner_hbm, node_hbm, cur_o, slots_o, outbox, turned, disp, owner, node, sems):
    copies = [
        pltpu.make_async_copy(src, dst, sems.at[i])
        for i, (src, dst) in enumerate(((owner_hbm, owner), (node_hbm, node), (disp_hbm, disp)))
    ]
    for copy in copies:
        copy.start()
    before = jnp.where(
        iota_rows(LANES, 2 * LANES) < lax.broadcasted_iota(i32, (LANES, 2 * LANES), 1), 1.0, 0.0
    ).astype(bf16)
    copies[0].wait()
    copies[1].wait()
    blocks = owner.shape[0]
    hots = [one_hot(owner[b : b + 1, :]) for b in range(blocks)]
    counts = jnp.dot(jnp.concatenate(hots, axis=0), before, preferred_element_type=f32)
    carry = jnp.zeros((LANES, LANES), f32)
    ranks = []
    for b in range(blocks):
        here = counts[b * LANES : (b + 1) * LANES]
        mine = iota_rows(LANES, LANES) == owner[b : b + 1, :]
        ranks.append(total(jnp.where(mine, carry + here[:, :LANES], 0.0)))
        carry = carry + here[:, LANES:]
    at = beside([node[b : b + 1, :] for b in range(blocks)])
    mask = matches(beside(ranks).astype(i32), OWN)
    zero = jnp.zeros((), bf16)
    put = jnp.concatenate(
        [jnp.where(mask, v.astype(f32).astype(bf16), zero) for v in (at & 127, (at >> 7) + 1)], axis=0
    )
    acc = lax.dot_general(put, beside(hots), (((1,), (1,)), ((), ())), preferred_element_type=f32)
    found = acc.astype(i32)
    slots_o[:OWN, :] = found[:OWN]
    slots_o[OWN:, :] = found[OWN:] - 1
    copies[2].wait()
    fold(disp, cur_o)
    fill_outbox(cur_o[...], slots_o, turned, outbox)


def groups(nodes, size):
    return [range(k, min(k + size, nodes)) for k in range(0, nodes, size)]


def element_fields(table, links, ue, rows, low, first, count, size):
    nodes = links.shape[0]
    few = rows < OWN
    both = jnp.concatenate(split(table), axis=0) if few else side_by_side(table)
    cols = slice(first, first + count)
    for group in groups(nodes, size):
        at = beside([links[k : k + 1, cols] for k in group])
        got = (pick_few if few else pick)(both, at & 127, (at >> 7) - low, rows)
        for c in range(3):
            row = total(got[c])
            for i, k in enumerate(group):
                ue[c * nodes + k : c * nodes + k + 1, :] = row[:, i * count : (i + 1) * count]


def stiff_times(stiff, ue):
    u_head, u_tail = split(ue[...])
    k_head, k_tail = split(stiff[...])
    dot = lambda a, b: jnp.dot(a, b, preferred_element_type=f32)
    twice = dot(k_head, beside([u_head, u_tail]))
    count = ue.shape[1]
    return twice[:, :count] + twice[:, count:] + dot(k_tail, u_head)


def put_pieces(force, fe):
    head = force.astype(bf16).astype(f32)
    fe[0] = head
    fe[1] = force - head


def element_sums(links, parts, rows, low, first, size):
    nodes = links.shape[0]
    cols = slice(first, first + sum(fe.shape[2] for fe in parts))
    acc = jnp.zeros((6 * rows, LANES), f32)
    for group in groups(nodes, size):
        at = beside([links[k : k + 1, cols] for k in group])
        values = [
            beside([fe[i, c * nodes + k : c * nodes + k + 1, :] for k in group for fe in parts])
            for i in range(2)
            for c in range(3)
        ]
        acc = acc + spread(values, at & 127, (at >> 7) - low, rows)
    return joined(acc)


def lend_kernel(table, lend, near, far):
    fill_messages(table[...], lend, near, far)


def rim_own_kernel(table, links, stiff, out, ue):
    count = links.shape[1] - INNER
    element_fields(table[...], links, ue, OWN, 0, INNER, count, 8)
    out[...] = stiff_times(stiff, ue)


def edges():
    me = lax.axis_index(AXES[0]) * lax.axis_size(AXES[1]) + lax.axis_index(AXES[1])
    last = lax.axis_size(AXES[0]) * lax.axis_size(AXES[1]) - 1
    return jnp.where(me > 0, 1.0, 0.0), jnp.where(me < last, 1.0, 0.0)


def rim_kernel(_, own, far, near, links, moduli, stiff, fe, back_far, back_near, ext, ue):
    low, high = edges()
    count = links.shape[1] - INNER
    lower, upper = by_parity(far[...], near[...]) * low, by_parity(near[...], far[...]) * high
    ext[...] = jnp.zeros(ext.shape, f32)
    for c in range(3):
        ext[c * GHOST : c * GHOST + 2, :] = lower[2 * c : 2 * c + 2, :]
        ext[c * GHOST + 2 : c * GHOST + 4, :] = upper[2 * c : 2 * c + 2, :]
    element_fields(ext[...], links, ue, GHOST, OWN, INNER, count, 8)
    put_pieces((own[...] + stiff_times(stiff, ue)) * moduli[:, INNER:], fe)
    ext[...] = element_sums(links, [fe], GHOST, OWN, INNER, 8)
    pad = jnp.zeros((2, LANES), f32)
    below = jnp.concatenate([ext[c * GHOST : c * GHOST + 2, :] for c in range(3)] + [pad], axis=0)
    above = jnp.concatenate([ext[c * GHOST + 2 : c * GHOST + 4, :] for c in range(3)] + [pad], axis=0)
    back_near[...] = by_parity(above, below)
    back_far[...] = by_parity(below, above)


def inner_kernel(rim_fe, table, links, moduli, stiff, out, ue, fe):
    element_fields(table[...], links, ue, OWN, 0, 0, INNER, 2)
    put_pieces(stiff_times(stiff, ue) * moduli[:, :INNER], fe)
    out[...] = element_sums(links, [fe, rim_fe], OWN, 0, 0, 2)


def first_inner_kernel(rim_fe, table, links, moduli, stiff, prev, load, out, prev_o, load_o, ue, fe):
    inner_kernel(rim_fe, table, links, moduli, stiff, out, ue, fe)
    fold(prev, prev_o)
    fold(load, load_o)


def pair_kernel(step, _, __, inbox, pairs, gap0, penalty, friction, slip, reply):
    both = side_by_side(inbox[...].T[: 3 * OWN])
    count = pairs.shape[1]
    wide = WIDE
    acc = jnp.zeros((6 * OWN, LANES), f32)
    for p in range(0, count, wide):
        cols = slice(p, p + wide)
        near, far = pairs[0:1, cols], pairs[1:2, cols]
        got_far = pick(both, far >> 5, far & 31, OWN)
        got_near = pick(both, near >> 5, near & 31, OWN)
        gap = [gap0[c : c + 1, cols] + total(got_far[c] - got_near[c]) for c in range(3)]
        stiff = penalty[:, cols]
        normal = stiff * jnp.maximum(-gap[2], 0.0)
        length = jnp.sqrt(gap[0] * gap[0] + gap[1] * gap[1] + 0.01)
        slide = -friction[:, cols] * normal / length
        factor = jnp.where(slip[step : step + 1, cols] == 1, slide, -0.5 * stiff)
        force = pieces([factor * gap[0], factor * gap[1], normal])
        both_ends = beside([far, near])
        force = [beside([v, -v]) for v in force]
        acc = acc + spread(force, both_ends >> 5, both_ends & 31, OWN)
    full = jnp.concatenate([joined(acc), jnp.zeros((LANES - 3 * OWN, LANES), f32)], axis=0)
    reply[...] = full.T


def contact_kernel(load, inner, returned, slots, out, turned):
    turned[...] = returned[...].T
    acc = jnp.zeros((6 * OWN, LANES), f32)
    for first in range(0, OWN, SLOTS):
        lo, hi = slot_rows(slots, first)
        rows = [
            beside([turned[c * OWN + r : c * OWN + r + 1, :] for r in range(first, first + SLOTS)])
            for c in range(3)
        ]
        acc = acc + spread(pieces(rows), lo, hi, OWN)
    out[...] = load[...] - inner[...] + joined(acc)


def new_state(cur, prev, mass, force, far, near, lend):
    near, far = near[...], far[...]
    low, high = edges()
    lower, upper = by_parity(far, near) * -low, by_parity(near, far) * -high
    node = beside([lend[0:1, :], lend[1:2, :]])
    rows = [
        beside([side[2 * c + i : 2 * c + i + 1, :] for side in (lower, upper) for i in range(2)]) for c in range(3)
    ]
    force = force[...] + joined(spread(pieces(rows), node & 127, node >> 7, OWN))
    weight = mass[...]
    acceleration = force / jnp.concatenate([weight, weight, weight], axis=0)
    return 2.0 * cur[...] - prev[...] + TIME_STEP_SQ * acceleration, acceleration


def update_kernel(cur, prev, mass, force, far, near, lend, slots, cur_o, outbox, turned):
    later, _ = new_state(cur, prev, mass, force, far, near, lend)
    cur_o[...] = later
    fill_outbox(later, slots, turned, outbox)


def last_kernel(cur, prev, mass, force, far, near, lend, disp_o, acc_o, held):
    later, acceleration = new_state(cur, prev, mass, force, far, near, lend)
    for value, out in ((later, disp_o), (acceleration, acc_o)):
        held[...] = value
        for c in range(3):
            for h in range(OWN):
                out[c : c + 1, h * LANES : (h + 1) * LANES] = held[c * OWN + h : c * OWN + h + 1, :]


def call(kernel, outs, scratch, flops, *args, outside=(), hbm=(), vmem=32):
    shapes = tuple(jax.ShapeDtypeStruct(s, t) for s, t in outs)
    space, anywhere = pl.BlockSpec(memory_space=pltpu.VMEM), pl.BlockSpec(memory_space=pl.ANY)
    in_hbm = pl.BlockSpec(memory_space=pltpu.HBM)
    return pl.pallas_call(
        kernel,
        out_shape=shapes,
        in_specs=[in_hbm if i in hbm else anywhere if i in outside else space for i in range(len(args))],
        out_specs=tuple(space for _ in shapes),
        scratch_shapes=[pltpu.VMEM(s, f32) if isinstance(s, tuple) else s for s in scratch],
        compiler_params=pltpu.CompilerParams(vmem_limit_bytes=vmem * 2**20),
        cost_estimate=pl.CostEstimate(flops=flops, bytes_accessed=2**20, transcendentals=0),
    )(*args)


def on_device(
    displacement,
    disp_prev,
    nodal_load,
    nodal_mass,
    modulus,
    stiffness,
    connectivity,
    ghost_send,
    contact_node,
    contact_owner,
    pair_ids,
    gap_start,
    penalty,
    friction,
    slip_state,
):
    devices = lax.axis_size(AXES)
    near_pairs = [(i, i ^ 1) for i in range(devices)]
    far_pairs = [(i, (i + 2 * (i % 2) - 1) % devices) for i in range(devices)]
    nodes = connectivity.shape[0]
    mass = nodal_mass.reshape(OWN, LANES)
    moduli = modulus.reshape(1, -1)
    stiff_pair, rub = penalty.reshape(1, -1), friction.reshape(1, -1)
    owner, node = contact_owner.reshape(-1, LANES), contact_node.reshape(-1, LANES)
    table, message, square = ((3 * OWN, LANES), f32), ((8, LANES), f32), ((LANES, LANES), f32)
    turned = (LANES, LANES)

    def swap(x):
        return lax.all_to_all(x, AXES, split_axis=0, concat_axis=0, tiled=True)

    cur, slots, outbox = call(
        begin_kernel,
        (table, ((2 * OWN, LANES), i32), square),
        (
            turned,
            displacement.shape,
            pltpu.VMEM(owner.shape, i32),
            pltpu.VMEM(node.shape, i32),
            pltpu.SemaphoreType.DMA((3,)),
        ),
        COST,
        displacement, owner, node,
        hbm=(0, 1, 2),
        vmem=60,
    )
    prev = load = None
    rim_count = connectivity.shape[1] - INNER
    rows = connectivity.shape[0] * 3
    for step in range(STEPS):
        inbox = swap(outbox)
        near, far = call(lend_kernel, (message, message), (), LONG, cur, ghost_send)
        lent = near
        near = lax.ppermute(near, AXES, near_pairs)
        far = lax.ppermute(far, AXES, far_pairs)
        (rim_own,) = call(
            rim_own_kernel,
            (((rows, rim_count), f32),),
            ((rows, rim_count),),
            LONG,
            cur, connectivity, stiffness,
        )
        (reply,) = call(
            lambda *refs, step=step: pair_kernel(step, *refs),
            (square,),
            (),
            LONG,
            lent, rim_own, inbox, pair_ids, gap_start, stiff_pair, rub, slip_state,
            outside=(0, 1),
        )
        rim, far, near = call(
            rim_kernel,
            (((2, rows, rim_count), f32), message, message),
            ((3 * GHOST, LANES), (rows, rim_count)),
            LONG,
            reply, rim_own, far, near, connectivity, moduli, stiffness,
            outside=(0,),
        )
        far = lax.ppermute(far, AXES, far_pairs)
        near = lax.ppermute(near, AXES, near_pairs)
        inner_scratch = ((rows, INNER), (2, rows, INNER))
        inner_args = (rim, cur, connectivity, moduli, stiffness)
        if step == 0:
            inner, prev, load = call(
                first_inner_kernel,
                (table, table, table),
                inner_scratch,
                COST,
                *inner_args, disp_prev, nodal_load,
            )
        else:
            (inner,) = call(inner_kernel, (table,), inner_scratch, COST, *inner_args)
        returned = swap(reply)
        (force,) = call(contact_kernel, (table,), (turned,), COST, load, inner, returned, slots)
        state = (cur, prev, mass, force, far, near, ghost_send)
        if step < STEPS - 1:
            later, outbox = call(update_kernel, (table, square), (turned,), COST, *state, slots)
            prev, cur = cur, later
        else:
            whole = (displacement.shape, f32)
            return call(last_kernel, (whole, whole), (table[0],), COST, *state)


def solution(mesh):
    row, flat = P(None, AXES), P(AXES)
    return jax.shard_map(
        on_device,
        mesh=mesh,
        in_specs=(row, row, row, flat, flat, P(), row, row, flat, flat, row, row, flat, flat, row),
        out_specs=(row, row),
        check_vma=False,
    )
```

```python
import jax
import jax.numpy as jnp
from jax import lax
from jax.experimental import pallas as pl
from jax.experimental.pallas import tpu as pltpu
from jax.sharding import PartitionSpec as P

AXES = ("px", "py")
STEPS = 3
TIME_STEP_SQ = 0.05
LANES = 128
OWN = 32
GHOST = 16
SLOTS = 8
WIDE = 1024
INNER = 384
COST, LONG = 10**6, 10**9
f32, bf16, i32 = jnp.float32, jnp.bfloat16, jnp.int32


def iota_rows(rows, count):
    return lax.broadcasted_iota(i32, (rows, count), 0)


def split(x):
    head = x.astype(bf16)
    return head, (x - head.astype(f32)).astype(bf16)


def side_by_side(x):
    return jnp.concatenate(split(x), axis=1)


def matches(row, size):
    return iota_rows(size, row.shape[1]).astype(f32).astype(bf16) == row.astype(f32).astype(bf16)


def one_hot(row):
    return jnp.where(matches(row, LANES), jnp.ones((), bf16), jnp.zeros((), bf16))


def pick(table, lo, hi, rows):
    hot = one_hot(lo)
    rows_of = jnp.dot(table, jnp.concatenate([hot, hot], axis=0), preferred_element_type=f32)
    mask = iota_rows(rows, lo.shape[1]) == hi
    return [
        jnp.where(mask, rows_of[c * rows : (c + 1) * rows], 0.0) for c in range(3)
    ]


def pick_few(table, lo, hi, rows):
    rows_of = joined(jnp.dot(table, one_hot(lo), preferred_element_type=f32))
    mask = iota_rows(rows, lo.shape[1]) == hi
    return [
        jnp.where(mask, rows_of[c * rows : (c + 1) * rows], 0.0) for c in range(3)
    ]


def total(x):
    return jnp.sum(x, axis=0, keepdims=True)


def spread(values, lo, hi, rows):
    mask = matches(hi, rows)
    zero = jnp.zeros((), bf16)
    placed = jnp.concatenate([jnp.where(mask, v.astype(bf16), zero) for v in values], axis=0)
    return lax.dot_general(
        placed, one_hot(lo), (((1,), (1,)), ((), ())), preferred_element_type=f32
    )


def pieces(rows):
    heads = [r.astype(bf16).astype(f32) for r in rows]
    return heads + [r - h for r, h in zip(rows, heads)]


def joined(acc):
    half = acc.shape[0] // 2
    return acc[:half] + acc[half:]


def beside(rows):
    return jnp.concatenate(rows, axis=1) if len(rows) > 1 else rows[0]


def slot_rows(slots, first):
    ranks = range(first, first + SLOTS)
    return beside([slots[r : r + 1, :] for r in ranks]), beside([slots[OWN + r : OWN + r + 1, :] for r in ranks])


def fill_outbox(table, slots, turned, outbox):
    both = side_by_side(table)
    turned[3 * OWN :, :] = jnp.zeros((LANES - 3 * OWN, LANES), f32)
    for first in range(0, OWN, SLOTS):
        lo, hi = slot_rows(slots, first)
        got = pick(both, lo, hi, OWN)
        for c in range(3):
            row = total(got[c])
            for i in range(SLOTS):
                at = c * OWN + first + i
                turned[at : at + 1, :] = row[:, i * LANES : (i + 1) * LANES]
    outbox[...] = turned[...].T


def odd():
    return lax.axis_index(AXES[1]) % 2 == 1


def by_parity(for_even, for_odd):
    return jnp.where(odd(), for_odd, for_even)


def fill_messages(table, lend, near, far):
    both = side_by_side(table)
    down, up = lend[0:1, :], lend[1:2, :]
    for node, message in ((by_parity(up, down), near), (by_parity(down, up), far)):
        got = pick(both, node & 127, node >> 7, OWN)
        message[6:8, :] = jnp.zeros((2, LANES), f32)
        for c in range(3):
            row = total(got[c])
            message[2 * c : 2 * c + 1, :] = row[:, :LANES]
            message[2 * c + 1 : 2 * c + 2, :] = row[:, LANES:]


def fold(src, dst):
    for c in range(3):
        for h in range(OWN):
            dst[c * OWN + h : c * OWN + h + 1, :] = src[c : c + 1, h * LANES : (h + 1) * LANES]


def begin_kernel(disp_hbm, owner_hbm, node_hbm, cur_o, slots_o, outbox, turned, disp, owner, node, sems):
    copies = [
        pltpu.make_async_copy(src, dst, sems.at[i])
        for i, (src, dst) in enumerate(((owner_hbm, owner), (node_hbm, node), (disp_hbm, disp)))
    ]
    for copy in copies:
        copy.start()
    before = jnp.where(
        iota_rows(LANES, 2 * LANES) < lax.broadcasted_iota(i32, (LANES, 2 * LANES), 1), 1.0, 0.0
    ).astype(bf16)
    copies[0].wait()
    copies[1].wait()
    blocks = owner.shape[0]
    hots = [one_hot(owner[b : b + 1, :]) for b in range(blocks)]
    counts = jnp.dot(jnp.concatenate(hots, axis=0), before, preferred_element_type=f32)
    carry = jnp.zeros((LANES, LANES), f32)
    ranks = []
    for b in range(blocks):
        here = counts[b * LANES : (b + 1) * LANES]
        mine = iota_rows(LANES, LANES) == owner[b : b + 1, :]
        ranks.append(total(jnp.where(mine, carry + here[:, :LANES], 0.0)))
        carry = carry + here[:, LANES:]
    at = beside([node[b : b + 1, :] for b in range(blocks)])
    mask = matches(beside(ranks).astype(i32), OWN)
    zero = jnp.zeros((), bf16)
    put = jnp.concatenate(
        [jnp.where(mask, v.astype(f32).astype(bf16), zero) for v in (at & 127, (at >> 7) + 1)], axis=0
    )
    acc = lax.dot_general(put, beside(hots), (((1,), (1,)), ((), ())), preferred_element_type=f32)
    found = acc.astype(i32)
    slots_o[:OWN, :] = found[:OWN]
    slots_o[OWN:, :] = found[OWN:] - 1
    copies[2].wait()
    fold(disp, cur_o)
    fill_outbox(cur_o[...], slots_o, turned, outbox)


def groups(nodes, size):
    return [range(k, min(k + size, nodes)) for k in range(0, nodes, size)]


def element_fields(table, links, ue, rows, low, first, count, size):
    nodes = links.shape[0]
    few = rows < OWN
    both = jnp.concatenate(split(table), axis=0) if few else side_by_side(table)
    cols = slice(first, first + count)
    for group in groups(nodes, size):
        at = beside([links[k : k + 1, cols] for k in group])
        got = (pick_few if few else pick)(both, at & 127, (at >> 7) - low, rows)
        for c in range(3):
            row = total(got[c])
            for i, k in enumerate(group):
                ue[c * nodes + k : c * nodes + k + 1, :] = row[:, i * count : (i + 1) * count]


def stiff_times(stiff, ue):
    u_head, u_tail = split(ue[...])
    k_head, k_tail = split(stiff[...])
    dot = lambda a, b: jnp.dot(a, b, preferred_element_type=f32)
    twice = dot(k_head, beside([u_head, u_tail]))
    count = ue.shape[1]
    return twice[:, :count] + twice[:, count:] + dot(k_tail, u_head)


def put_pieces(force, fe):
    head = force.astype(bf16).astype(f32)
    fe[0] = head
    fe[1] = force - head


def element_sums(links, parts, rows, low, first, size):
    nodes = links.shape[0]
    cols = slice(first, first + sum(fe.shape[2] for fe in parts))
    acc = jnp.zeros((6 * rows, LANES), f32)
    for group in groups(nodes, size):
        at = beside([links[k : k + 1, cols] for k in group])
        values = [
            beside([fe[i, c * nodes + k : c * nodes + k + 1, :] for k in group for fe in parts])
            for i in range(2)
            for c in range(3)
        ]
        acc = acc + spread(values, at & 127, (at >> 7) - low, rows)
    return joined(acc)


def lend_kernel(table, lend, near, far):
    fill_messages(table[...], lend, near, far)


def rim_own_kernel(table, links, stiff, out, ue):
    count = links.shape[1] - INNER
    element_fields(table[...], links, ue, OWN, 0, INNER, count, 8)
    out[...] = stiff_times(stiff, ue)


def edges():
    me = lax.axis_index(AXES[0]) * lax.axis_size(AXES[1]) + lax.axis_index(AXES[1])
    last = lax.axis_size(AXES[0]) * lax.axis_size(AXES[1]) - 1
    return jnp.where(me > 0, 1.0, 0.0), jnp.where(me < last, 1.0, 0.0)


def rim_kernel(_, own, far, near, links, moduli, stiff, fe, back_far, back_near, ext, ue):
    low, high = edges()
    count = links.shape[1] - INNER
    lower, upper = by_parity(far[...], near[...]) * low, by_parity(near[...], far[...]) * high
    ext[...] = jnp.zeros(ext.shape, f32)
    for c in range(3):
        ext[c * GHOST : c * GHOST + 2, :] = lower[2 * c : 2 * c + 2, :]
        ext[c * GHOST + 2 : c * GHOST + 4, :] = upper[2 * c : 2 * c + 2, :]
    element_fields(ext[...], links, ue, GHOST, OWN, INNER, count, 8)
    put_pieces((own[...] + stiff_times(stiff, ue)) * moduli[:, INNER:], fe)
    ext[...] = element_sums(links, [fe], GHOST, OWN, INNER, 8)
    pad = jnp.zeros((2, LANES), f32)
    below = jnp.concatenate([ext[c * GHOST : c * GHOST + 2, :] for c in range(3)] + [pad], axis=0)
    above = jnp.concatenate([ext[c * GHOST + 2 : c * GHOST + 4, :] for c in range(3)] + [pad], axis=0)
    back_near[...] = by_parity(above, below)
    back_far[...] = by_parity(below, above)


def inner_kernel(rim_fe, table, links, moduli, stiff, out, ue, fe):
    element_fields(table[...], links, ue, OWN, 0, 0, INNER, 4)
    put_pieces(stiff_times(stiff, ue) * moduli[:, :INNER], fe)
    out[...] = element_sums(links, [fe, rim_fe], OWN, 0, 0, 4)


def first_inner_kernel(rim_fe, table, links, moduli, stiff, prev, load, out, prev_o, load_o, ue, fe):
    inner_kernel(rim_fe, table, links, moduli, stiff, out, ue, fe)
    fold(prev, prev_o)
    fold(load, load_o)


def pair_kernel(step, _, __, inbox, pairs, gap0, penalty, friction, slip, reply):
    both = side_by_side(inbox[...].T[: 3 * OWN])
    count = pairs.shape[1]
    wide = WIDE
    acc = jnp.zeros((6 * OWN, LANES), f32)
    for p in range(0, count, wide):
        cols = slice(p, p + wide)
        near, far = pairs[0:1, cols], pairs[1:2, cols]
        got_far = pick(both, far >> 5, far & 31, OWN)
        got_near = pick(both, near >> 5, near & 31, OWN)
        gap = [gap0[c : c + 1, cols] + total(got_far[c] - got_near[c]) for c in range(3)]
        stiff = penalty[:, cols]
        normal = stiff * jnp.maximum(-gap[2], 0.0)
        length = jnp.sqrt(gap[0] * gap[0] + gap[1] * gap[1] + 0.01)
        slide = -friction[:, cols] * normal / length
        factor = jnp.where(slip[step : step + 1, cols] == 1, slide, -0.5 * stiff)
        force = pieces([factor * gap[0], factor * gap[1], normal])
        both_ends = beside([far, near])
        force = [beside([v, -v]) for v in force]
        acc = acc + spread(force, both_ends >> 5, both_ends & 31, OWN)
    full = jnp.concatenate([joined(acc), jnp.zeros((LANES - 3 * OWN, LANES), f32)], axis=0)
    reply[...] = full.T


def contact_kernel(load, inner, returned, slots, out, turned):
    turned[...] = returned[...].T
    acc = jnp.zeros((6 * OWN, LANES), f32)
    for first in range(0, OWN, SLOTS):
        lo, hi = slot_rows(slots, first)
        rows = [
            beside([turned[c * OWN + r : c * OWN + r + 1, :] for r in range(first, first + SLOTS)])
            for c in range(3)
        ]
        acc = acc + spread(pieces(rows), lo, hi, OWN)
    out[...] = load[...] - inner[...] + joined(acc)


def new_state(cur, prev, mass, force, far, near, lend):
    near, far = near[...], far[...]
    low, high = edges()
    lower, upper = by_parity(far, near) * -low, by_parity(near, far) * -high
    node = beside([lend[0:1, :], lend[1:2, :]])
    rows = [
        beside([side[2 * c + i : 2 * c + i + 1, :] for side in (lower, upper) for i in range(2)]) for c in range(3)
    ]
    force = force[...] + joined(spread(pieces(rows), node & 127, node >> 7, OWN))
    weight = mass[...]
    acceleration = force / jnp.concatenate([weight, weight, weight], axis=0)
    return 2.0 * cur[...] - prev[...] + TIME_STEP_SQ * acceleration, acceleration


def update_kernel(cur, prev, mass, force, far, near, lend, slots, cur_o, outbox, turned):
    later, _ = new_state(cur, prev, mass, force, far, near, lend)
    cur_o[...] = later
    fill_outbox(later, slots, turned, outbox)


def last_kernel(cur, prev, mass, force, far, near, lend, disp_o, acc_o, held):
    later, acceleration = new_state(cur, prev, mass, force, far, near, lend)
    for value, out in ((later, disp_o), (acceleration, acc_o)):
        held[...] = value
        for c in range(3):
            for h in range(OWN):
                out[c : c + 1, h * LANES : (h + 1) * LANES] = held[c * OWN + h : c * OWN + h + 1, :]


def call(kernel, outs, scratch, flops, *args, outside=(), hbm=(), vmem=32):
    shapes = tuple(jax.ShapeDtypeStruct(s, t) for s, t in outs)
    space, anywhere = pl.BlockSpec(memory_space=pltpu.VMEM), pl.BlockSpec(memory_space=pl.ANY)
    in_hbm = pl.BlockSpec(memory_space=pltpu.HBM)
    return pl.pallas_call(
        kernel,
        out_shape=shapes,
        in_specs=[in_hbm if i in hbm else anywhere if i in outside else space for i in range(len(args))],
        out_specs=tuple(space for _ in shapes),
        scratch_shapes=[pltpu.VMEM(s, f32) if isinstance(s, tuple) else s for s in scratch],
        compiler_params=pltpu.CompilerParams(vmem_limit_bytes=vmem * 2**20),
        cost_estimate=pl.CostEstimate(flops=flops, bytes_accessed=2**20, transcendentals=0),
    )(*args)


def on_device(
    displacement,
    disp_prev,
    nodal_load,
    nodal_mass,
    modulus,
    stiffness,
    connectivity,
    ghost_send,
    contact_node,
    contact_owner,
    pair_ids,
    gap_start,
    penalty,
    friction,
    slip_state,
):
    devices = lax.axis_size(AXES)
    near_pairs = [(i, i ^ 1) for i in range(devices)]
    far_pairs = [(i, (i + 2 * (i % 2) - 1) % devices) for i in range(devices)]
    nodes = connectivity.shape[0]
    mass = nodal_mass.reshape(OWN, LANES)
    moduli = modulus.reshape(1, -1)
    stiff_pair, rub = penalty.reshape(1, -1), friction.reshape(1, -1)
    owner, node = contact_owner.reshape(-1, LANES), contact_node.reshape(-1, LANES)
    table, message, square = ((3 * OWN, LANES), f32), ((8, LANES), f32), ((LANES, LANES), f32)
    turned = (LANES, LANES)

    def swap(x):
        return lax.all_to_all(x, AXES, split_axis=0, concat_axis=0, tiled=True)

    cur, slots, outbox = call(
        begin_kernel,
        (table, ((2 * OWN, LANES), i32), square),
        (
            turned,
            displacement.shape,
            pltpu.VMEM(owner.shape, i32),
            pltpu.VMEM(node.shape, i32),
            pltpu.SemaphoreType.DMA((3,)),
        ),
        COST,
        displacement, owner, node,
        hbm=(0, 1, 2),
        vmem=60,
    )
    prev = load = None
    rim_count = connectivity.shape[1] - INNER
    rows = connectivity.shape[0] * 3
    for step in range(STEPS):
        inbox = swap(outbox)
        near, far = call(lend_kernel, (message, message), (), LONG, cur, ghost_send)
        lent = near
        near = lax.ppermute(near, AXES, near_pairs)
        far = lax.ppermute(far, AXES, far_pairs)
        (rim_own,) = call(
            rim_own_kernel,
            (((rows, rim_count), f32),),
            ((rows, rim_count),),
            LONG,
            cur, connectivity, stiffness,
        )
        (reply,) = call(
            lambda *refs, step=step: pair_kernel(step, *refs),
            (square,),
            (),
            LONG,
            lent, rim_own, inbox, pair_ids, gap_start, stiff_pair, rub, slip_state,
            outside=(0, 1),
        )
        rim, far, near = call(
            rim_kernel,
            (((2, rows, rim_count), f32), message, message),
            ((3 * GHOST, LANES), (rows, rim_count)),
            LONG,
            reply, rim_own, far, near, connectivity, moduli, stiffness,
            outside=(0,),
        )
        far = lax.ppermute(far, AXES, far_pairs)
        near = lax.ppermute(near, AXES, near_pairs)
        inner_scratch = ((rows, INNER), (2, rows, INNER))
        inner_args = (rim, cur, connectivity, moduli, stiffness)
        if step == 0:
            inner, prev, load = call(
                first_inner_kernel,
                (table, table, table),
                inner_scratch,
                COST,
                *inner_args, disp_prev, nodal_load,
            )
        else:
            (inner,) = call(inner_kernel, (table,), inner_scratch, COST, *inner_args)
        returned = swap(reply)
        (force,) = call(contact_kernel, (table,), (turned,), COST, load, inner, returned, slots)
        state = (cur, prev, mass, force, far, near, ghost_send)
        if step < STEPS - 1:
            later, outbox = call(update_kernel, (table, square), (turned,), COST, *state, slots)
            prev, cur = cur, later
        else:
            whole = (displacement.shape, f32)
            return call(last_kernel, (whole, whole), (table[0],), COST, *state)


def solution(mesh):
    row, flat = P(None, AXES), P(AXES)
    return jax.shard_map(
        on_device,
        mesh=mesh,
        in_specs=(row, row, row, flat, flat, P(), row, row, flat, flat, row, row, flat, flat, row),
        out_specs=(row, row),
        check_vma=False,
    )
```
